32 devices in a mesh: member: 2 (over y), mesh: 16 (over z, x, core).
Axes of the slice: x: 2, y: 2, z: 4, core: 2. Of those that a mesh axis runs over, the one named last changes fastest.
Arguments:
- struct_modes: bfloat16 [24576, 2048], P(('member', 'mesh')), parts along dimension 0, may hold values from -0.078125 to 0.078125
- acoustic_modes: bfloat16 [16384, 2048], P(('member', 'mesh')), parts along dimension 0, may hold values from -6 to 6
- coupling: bfloat16 [320, 64, 256], P('mesh'), may hold values from -0.375 to 0.375
- face_shift: int32 [192], P('mesh'), may hold values from 0 to 4, as said below
- face_blocks: int32 [320, 4], P('mesh'), may hold values from 0 to 7
Outputs:
- panel: float32 [4096, 2048], P(('member', 'mesh')), parts along dimension 0
The draws below stay inside these ranges and needn't reach their ends.
There are 2 independent parts, one for each index of `member`. The reference program is written for one: setup_inputs(seed, part) draws one part's arguments, and reference() takes and returns one part's arrays. A program takes and returns all parts, laid end to end along the dimension named above; an argument that names none is the same for every part. Nothing has to cross between parts.
Inputs may be any that keep to these rules, and one draw needn't show every extreme that they name: `face_shift`: on each shell owner the counts of its 12 blocks over the five classes are a reordering of 4, 1, 3, 2 and 2; so no shell owner hands more than 4 blocks to one face owner, and a face owner receives at most 4 from each of its five shell owners (at most 20 in all); in every draw at least one face owner receives exactly 4 from each of its five shell owners.
All inputs are finite; a program needn't handle non-finite values.
Results may differ from the reference program's by a relative error of at most 0.0029.
Values may be sent and summed in bfloat16 or wider, within the bound.
No kernel may reach another device: no remote copies, remote signals or barrier semaphores. Data moves between devices by JAX's collectives and lax.ppermute only.
A program may use at most 128 MiB of HBM per device.

```python
import jax
import jax.numpy as jnp
from jax import lax

MS = 2048
MA = 2048
BW = 64
NNZ = 4
CAP = 4
SB_DEV = 12
AB_DEV = 8
SBLK = 192
ABLK = 128
FACE_SLOTS = 320
N_MESH = 16


def draw_face_shift(key, part):
    base_counts = jnp.array([4, 1, 3, 2, 2], jnp.int32) * (CAP // 4)
    device_keys = jax.random.split(jax.random.fold_in(key, 11), N_MESH)
    order = jax.vmap(lambda k: jax.random.permutation(k, 5))(device_keys).astype(jnp.int32)
    target = jax.random.randint(jax.random.fold_in(key, 12), (), 0, N_MESH)
    devices = jnp.arange(N_MESH, dtype=jnp.int32)
    distance = (devices - target + 2) % N_MESH
    inside = distance < 5
    column = jnp.clip(4 - distance, 0, 4)
    zero_at = jnp.argmin(order, axis=1)
    value_there = jnp.take_along_axis(order, column[:, None], axis=1)
    positions = jnp.arange(5, dtype=jnp.int32)[None, :]
    swapped = jnp.where(positions == column[:, None], 0, jnp.where(positions == zero_at[:, None], value_there, order))
    order = jnp.where(inside[:, None], swapped, order)
    counts = base_counts[order]
    ends = jnp.cumsum(counts, axis=1)
    places = jnp.arange(SB_DEV, dtype=jnp.int32)
    classes = jnp.sum((places[None, :, None] >= ends[:, None, :4]).astype(jnp.int32), axis=2)
    shuffle_keys = jax.random.split(jax.random.fold_in(key, 13), N_MESH)
    shuffled = jax.vmap(lambda k, row: jax.random.permutation(k, row))(shuffle_keys, classes)
    return shuffled.reshape(-1).astype(jnp.int32)


def place_ends(result, rng, smallest, largest):
    longest = result.shape.index(max(result.shape))
    spots = []
    for shift in (0, 1):
        where = [jax.random.randint(jax.random.fold_in(rng, axis), (), 0, length) for axis, length in enumerate(result.shape)]
        where[longest] = (where[longest] + shift) % result.shape[longest]
        spots.append(tuple(where))
    return result.at[spots[0]].set(smallest).at[spots[1]].set(largest)


def raised(entries, key, source, target, blocks, factor):
    owner, partner = [(jnp.arange(entries.shape[axis_at]) // (entries.shape[axis_at] // blocks)).reshape([-1 if axis == axis_at else 1 for axis in range(entries.ndim)]) for axis_at in (source, target)]
    chosen = jax.random.permutation(key, blocks)[partner]
    strong = (owner == chosen) | (owner == (partner + blocks // 2) % blocks)
    return jnp.where(strong, factor * entries, entries)


def level_of(rng, shape, cuts, smallest, largest):
    factor_of = 1.0
    for dim, blocks in cuts:
        heights = jax.random.uniform(jax.random.fold_in(jax.random.fold_in(rng, 6), dim), (blocks,), jnp.float32, smallest / len(cuts), largest / len(cuts))
        factor_of = factor_of * jnp.repeat(jnp.exp(heights), shape[dim] // blocks).reshape((-1,) + (1,) * (len(shape) - 1 - dim))
    return factor_of


def normal_values(own_key, dims, spread, reach, cuts=(), kind=jnp.bfloat16):
    drawn = spread * jax.random.normal(own_key, dims, jnp.float32)
    if cuts:
        drawn = drawn * level_of(own_key, dims, cuts, -0.22, 0.18)
    return jnp.clip(drawn, -reach, reach).astype(kind)


def gaussian_with(stream_key, dims, deviation, most, shards, heavy, held_as=jnp.bfloat16):
    drawn = deviation * jax.random.normal(stream_key, dims, jnp.float32)
    if shards:
        drawn = drawn * level_of(stream_key, dims, shards, -0.22, 0.18)
    return jnp.clip(raised(drawn, jax.random.fold_in(stream_key, 3), *heavy), -most, most).astype(held_as)


def setup_inputs(seed: int = 0, part: int = 0) -> dict:
    streams_of = jax.random.split(jax.random.key(seed), 6)
    part_splits = jax.random.split(jax.random.fold_in(streams_of[5], part), 6)
    struct_modes = gaussian_with(part_splits[0], (SBLK * BW, MS), (SBLK * BW) ** -0.5, 0.078125, ((0, 16),), (0, 1, 16, 2.0))
    acoustic_modes = normal_values(part_splits[1], (ABLK * BW, MA), 1.0, 6.0, ((0, 16),))
    coupling = normal_values(streams_of[2], (FACE_SLOTS, BW, NNZ * BW), (NNZ * BW) ** -0.5, 0.375, ((0, 16),))
    face_shift = draw_face_shift(jax.random.fold_in(streams_of[5], 71), part)
    face_blocks = place_ends(jax.random.randint(streams_of[4], (FACE_SLOTS, NNZ), 0, AB_DEV), jax.random.fold_in(streams_of[4], 1), 0, AB_DEV - 1).astype(jnp.int32)
    return {"struct_modes": struct_modes, "acoustic_modes": acoustic_modes, "coupling": coupling, "face_shift": face_shift, "face_blocks": face_blocks}


def reference(struct_modes, acoustic_modes, coupling, face_shift, face_blocks):
    slot_count = 5 * CAP
    shell_shift = face_shift.reshape(N_MESH, SB_DEV)
    classes = jnp.arange(5, dtype=jnp.int32)
    onehot = (shell_shift[:, :, None] == classes[None, None, :]).astype(jnp.int32)
    before = jnp.cumsum(onehot, axis=1) - onehot
    slot_index = jnp.sum(before * onehot, axis=2).reshape(-1)
    shell_owner = jnp.arange(SBLK, dtype=jnp.int32) // SB_DEV
    face_owner = (shell_owner + face_shift - 2) % N_MESH
    coupling_row = (face_owner * slot_count + face_shift * CAP + slot_index).astype(jnp.int32)
    acoustic_blocks = acoustic_modes.reshape(ABLK, BW, MA)

    def coupled(target_pair):
        target, owner = target_pair
        picked = acoustic_blocks[(owner * AB_DEV + face_blocks[target]).astype(jnp.int32)].reshape(NNZ * BW, MA)
        return jnp.dot(coupling[target], picked, preferred_element_type=jnp.float32).astype(jnp.bfloat16)

    coupled_rows = lax.map(coupled, (coupling_row, face_owner.astype(jnp.int32))).reshape(SBLK * BW, MA)
    return lax.dot_general(struct_modes, coupled_rows, (((0,), (0,)), ((), ())), preferred_element_type=jnp.float32)
```

```python
import functools

import jax
import jax.numpy as jnp
from jax import lax
from jax.experimental import pallas as pl
from jax.experimental.pallas import tpu as pltpu
from jax.sharding import PartitionSpec as P

CLASSES = 5
CHUNKS = 4


def coupled_kernel(blocks_ref, acoustic_ref, coupling_ref, *refs):
    outs, picked = refs[:CLASSES], refs[CLASSES]
    slots, rows, depth = coupling_ref.shape
    per_class = slots // CLASSES
    for slot in range(slots):
        for n in range(depth // rows):
            at = pl.multiple_of(blocks_ref[slot, n] * rows, rows)
            picked[n * rows : (n + 1) * rows, :] = acoustic_ref[pl.ds(at, rows), :]
        product = jnp.dot(
            coupling_ref[slot], picked[...], preferred_element_type=jnp.float32
        )
        k, s = divmod(slot, per_class)
        outs[k][s * rows : (s + 1) * rows, :] = product.astype(jnp.bfloat16)


def coupled_chunk(blocks, acoustic, coupling, chunk, width):
    slots, rows, depth = coupling.shape
    tall = slots // CLASSES * rows
    return pl.pallas_call(
        coupled_kernel,
        out_shape=[jax.ShapeDtypeStruct((tall, width), jnp.bfloat16)] * CLASSES,
        grid_spec=pltpu.PrefetchScalarGridSpec(
            num_scalar_prefetch=1,
            grid=(1,),
            in_specs=[
                pl.BlockSpec((acoustic.shape[0], width), lambda i, b: (0, chunk)),
                pl.BlockSpec(coupling.shape, lambda i, b: (0, 0, 0)),
            ],
            out_specs=[pl.BlockSpec((tall, width), lambda i, b: (0, 0))] * CLASSES,
            scratch_shapes=[pltpu.VMEM((depth, width), jnp.bfloat16)],
        ),
        compiler_params=pltpu.CompilerParams(vmem_limit_bytes=32 * 2**20),
        cost_estimate=pl.CostEstimate(
            flops=2 * slots * rows * depth * width,
            bytes_accessed=2 * width * (acoustic.shape[0] + slots * rows),
            transcendentals=0,
        ),
        name="coupled_chunk",
    )(blocks, acoustic, coupling)


def panel_kernel(shift_ref, left_ref, *refs):
    pieces, out_ref, picked = refs[:CLASSES], refs[CLASSES], refs[CLASSES + 1]
    count = shift_ref.shape[0]
    rows = left_ref.shape[1] // count

    @pl.when(pl.program_id(0) == 0)
    def _():
        seen = [jnp.int32(0)] * CLASSES
        for b in range(count):
            kind = shift_ref[b]
            slot = jnp.int32(0)
            for k in range(CLASSES):
                slot = jnp.where(kind == k, seen[k], slot)
                seen[k] = seen[k] + (kind == k).astype(jnp.int32)
            at = pl.multiple_of(slot * rows, rows)
            for k in range(CLASSES):

                @pl.when(kind == k)
                def _(k=k, b=b, at=at):
                    picked[b * rows : (b + 1) * rows, :] = pieces[k][pl.ds(at, rows), :]

    out_ref[...] = jnp.dot(
        left_ref[...], picked[...], preferred_element_type=jnp.float32
    ).astype(out_ref.dtype)


def panel_part(shift, left, pieces, dtype):
    tall, depth = left.shape
    high, width = pieces[0].shape
    tile = min(tall, 256)
    return pl.pallas_call(
        panel_kernel,
        out_shape=jax.ShapeDtypeStruct((tall, width), dtype),
        grid_spec=pltpu.PrefetchScalarGridSpec(
            num_scalar_prefetch=1,
            grid=(tall // tile,),
            in_specs=[pl.BlockSpec((tile, depth), lambda i, s: (i, 0))]
            + [pl.BlockSpec((high, width), lambda i, s: (0, 0))] * CLASSES,
            out_specs=pl.BlockSpec((tile, width), lambda i, s: (i, 0)),
            scratch_shapes=[pltpu.VMEM((depth, width), jnp.bfloat16)],
        ),
        compiler_params=pltpu.CompilerParams(vmem_limit_bytes=32 * 2**20),
        cost_estimate=pl.CostEstimate(
            flops=2 * tall * depth * width,
            bytes_accessed=2 * (tall * depth + CLASSES * high * width) + 4 * tall * width,
            transcendentals=0,
        ),
        name="panel_part",
    )(shift, left, *pieces)


def passed_along(block, distance):
    size = lax.axis_size("mesh")
    return lax.ppermute(block, "mesh", [((i - distance) % size, i) for i in range(size)])


def swapped(block, bit):
    size = lax.axis_size("mesh")
    return lax.ppermute(block, "mesh", [(i, i ^ (1 << bit)) for i in range(size)])


def halving_order(size):
    bits = list(range(size.bit_length() - 1))
    return [0, 2, 1] + bits[3:] if len(bits) > 2 else bits


def per_device(struct_modes, acoustic_modes, coupling, face_shift, face_blocks):
    size = lax.axis_size("mesh")
    me = lax.axis_index("mesh")
    width = acoustic_modes.shape[1] // CHUNKS
    share = struct_modes.shape[1] // size
    order = halving_order(size)

    sides = struct_modes.T.reshape(size // 2, 2, share, -1)
    mine = me & 1

    def side(which):
        return lax.dynamic_index_in_dim(sides, which, 1, keepdims=False).reshape(
            size // 2 * share, -1
        )

    kept_left, sent_left = side(mine), side(1 - mine)

    columns = []
    for chunk in range(CHUNKS):
        made = coupled_chunk(face_blocks, acoustic_modes, coupling, chunk, width)
        pieces = [
            made[k] if k == 2 else passed_along(made[k], 2 - k) for k in range(CLASSES)
        ]
        got = swapped(panel_part(face_shift, sent_left, pieces, jnp.bfloat16), order[0])
        held = panel_part(face_shift, kept_left, pieces, jnp.float32)
        left_bits = sorted(order[1:], reverse=True)
        for level, bit in enumerate(order[1:], 1):
            place = left_bits.index(bit)
            left_bits.remove(bit)
            total = (held + got.astype(jnp.float32)).reshape(2**place, 2, -1, width)
            here = (me >> bit) & 1
            held = lax.dynamic_index_in_dim(total, here, 1, keepdims=False)
            away = lax.dynamic_index_in_dim(total, 1 - here, 1, keepdims=False)
            held = held.reshape(-1, width)
            wire = jnp.bfloat16 if level < 4 else jnp.float32
            got = swapped(away.reshape(-1, width).astype(wire), bit)
        columns.append(held + got.astype(jnp.float32))
    return jnp.concatenate(columns, axis=1)


def solution(mesh):
    placed = (
        P(("member", "mesh"), None),
        P(("member", "mesh"), None),
        P("mesh", None, None),
        P("mesh"),
        P("mesh", None),
    )
    return jax.shard_map(
        per_device,
        mesh=mesh,
        in_specs=placed,
        out_specs=P(("member", "mesh"), None),
        check_vma=False,
    )
```

```python
import jax
import jax.numpy as jnp
from jax import lax
from jax.experimental import pallas as pl
from jax.experimental.pallas import tpu as pltpu
from jax.sharding import PartitionSpec as P

CLASSES = 5
EIGHTHS = (2, 2, 2, 1, 1)
LIMIT = 20 * 2**20
ANY = pl.BlockSpec(memory_space=pl.ANY)
BF16, F32 = jnp.bfloat16, jnp.float32


def call(body, scalars, arrays, specs, after, out_shape, out_specs, grid, scratch, flops, alias=None):
    lead = len(scalars) + len(arrays)
    extra = len(after)

    def kernel(*refs):
        body(*refs[:lead], *refs[lead + extra :])

    touched = sum(a.size * a.dtype.itemsize for a in arrays)
    aliases = {} if alias is None else {lead - 1: alias}
    return pl.pallas_call(
        kernel,
        out_shape=out_shape,
        grid_spec=pltpu.PrefetchScalarGridSpec(
            num_scalar_prefetch=len(scalars),
            grid=grid,
            in_specs=specs + [ANY] * extra,
            out_specs=out_specs,
            scratch_shapes=scratch,
        ),
        input_output_aliases=aliases,
        compiler_params=pltpu.CompilerParams(vmem_limit_bytes=LIMIT),
        cost_estimate=pl.CostEstimate(flops=flops, bytes_accessed=touched, transcendentals=0),
        name=body.__name__,
    )(*scalars, *arrays, *after)


def coupled(blocks, acoustic, coupling, classes, at, width, after):
    slots, rows, depth = coupling.shape
    per = slots // CLASSES

    def coupled_rows(blocks_ref, acoustic_ref, coupling_ref, *refs):
        outs, picked = refs[:-1], refs[-1]
        for k, out in zip(classes, outs):
            for s in range(per):
                slot = k * per + s
                for n in range(depth // rows):
                    first = pl.multiple_of(blocks_ref[slot, n] * rows, rows)
                    picked[n * rows : (n + 1) * rows, :] = acoustic_ref[pl.ds(first, rows), :]
                out[s * rows : (s + 1) * rows, :] = jnp.dot(
                    coupling_ref[slot], picked[...], preferred_element_type=F32
                ).astype(BF16)

    count = len(classes)
    return call(
        coupled_rows,
        [blocks],
        [acoustic, coupling],
        [
            pl.BlockSpec((acoustic.shape[0], width), lambda i, b: (0, at // width)),
            pl.BlockSpec(coupling.shape, lambda i, b: (0, 0, 0)),
        ],
        after,
        [jax.ShapeDtypeStruct((per * rows, width), BF16)] * count,
        [pl.BlockSpec((per * rows, width), lambda i, b: (0, 0))] * count,
        (1,),
        [pltpu.VMEM((depth, width), BF16)],
        2 * count * per * rows * depth * width,
    )


def turned(mine, struct_modes, share, after):
    depth, modes = struct_modes.shape
    half = modes // 2

    def turn(mine_ref, kept_ref, sent_ref, kept_out, sent_out):
        kept_out[...] = kept_ref[...].T
        sent_out[...] = sent_ref[...].T

    if share % 128:
        sides = struct_modes.T.reshape(-1, 2, share, depth)
        return tuple(
            lax.dynamic_index_in_dim(sides, side, 1, keepdims=False).reshape(half, depth)
            for side in (mine, 1 - mine)
        )
    return call(
        turn,
        [mine.reshape(1)],
        [struct_modes, struct_modes],
        [
            pl.BlockSpec((depth, share), lambda i, m: (0, 2 * i + m[0])),
            pl.BlockSpec((depth, share), lambda i, m: (0, 2 * i + 1 - m[0])),
        ],
        after,
        [jax.ShapeDtypeStruct((half, depth), BF16)] * 2,
        [pl.BlockSpec((share, depth), lambda i, m: (i, 0))] * 2,
        (half // share,),
        [],
        0,
    )


def panel_sent(shift, left, pieces, after):
    tall, depth = left.shape
    high, width = pieces[0].shape
    tile = min(tall, 256)

    def panel_away(shift_ref, left_ref, *refs):
        parts, out_ref, picked = refs[:CLASSES], refs[CLASSES], refs[CLASSES + 1]
        count = shift_ref.shape[0]
        rows = depth // count

        @pl.when(pl.program_id(0) == 0)
        def _():
            seen = [jnp.int32(0)] * CLASSES
            for b in range(count):
                kind = shift_ref[b]
                slot = jnp.int32(0)
                for k in range(CLASSES):
                    slot = jnp.where(kind == k, seen[k], slot)
                    seen[k] = seen[k] + (kind == k).astype(jnp.int32)
                first = pl.multiple_of(slot * rows, rows)
                for k in range(CLASSES):

                    @pl.when(kind == k)
                    def _(k=k, b=b, first=first):
                        picked[b * rows : (b + 1) * rows, :] = parts[k][pl.ds(first, rows), :]

        out_ref[...] = jnp.dot(left_ref[...], picked[...], preferred_element_type=F32).astype(BF16)

    return call(
        panel_away,
        [shift],
        [left, *pieces],
        [pl.BlockSpec((tile, depth), lambda i, s: (i, 0))]
        + [pl.BlockSpec((high, width), lambda i, s: (0, 0))] * CLASSES,
        after,
        [
            jax.ShapeDtypeStruct((tall, width), BF16),
            jax.ShapeDtypeStruct((depth, width), BF16),
        ],
        [
            pl.BlockSpec((tile, width), lambda i, s: (i, 0)),
            pl.BlockSpec((depth, width), lambda i, s: (0, 0)),
        ],
        (tall // tile,),
        [],
        2 * tall * depth * width,
    )


def panel_kept(left, picked, after):
    tall, depth = left.shape
    width = picked.shape[1]
    tile = min(tall, 256)

    def panel_own(left_ref, picked_ref, out_ref):
        out_ref[...] = jnp.dot(left_ref[...], picked_ref[...], preferred_element_type=F32)

    return call(
        panel_own,
        [],
        [left, picked],
        [
            pl.BlockSpec((tile, depth), lambda i: (i, 0)),
            pl.BlockSpec((depth, width), lambda i: (0, 0)),
        ],
        after,
        jax.ShapeDtypeStruct((tall, width), F32),
        pl.BlockSpec((tile, width), lambda i: (i, 0)),
        (tall // tile,),
        [],
        2 * tall * depth * width,
    )


def added(held, got, here, before, wire, after):
    width = held.shape[1]
    shape = (before, 2, held.shape[0] // before // 2, width)
    block = (1, *shape[1:])
    out = (shape[0] * shape[2], width)

    def added_split(here_ref, held_ref, got_ref, kept_ref, away_ref):
        side = here_ref[0]
        kept_ref[...] = held_ref[0, side] + got_ref[0, side].astype(F32)
        away_ref[...] = (held_ref[0, 1 - side] + got_ref[0, 1 - side].astype(F32)).astype(wire)

    return call(
        added_split,
        [here.reshape(1)],
        [held.reshape(shape), got.reshape(shape)],
        [pl.BlockSpec(block, lambda i, h: (i, 0, 0, 0))] * 2,
        after,
        [jax.ShapeDtypeStruct(out, F32), jax.ShapeDtypeStruct(out, wire)],
        [pl.BlockSpec(shape[2:], lambda i, h: (i, 0))] * 2,
        (before,),
        [],
        2 * held.size,
    )


def finished(held, got, buffer, at, modes, after):
    rows, width = held.shape

    def added_last(held_ref, got_ref, *refs):
        refs[-1][...] = held_ref[...] + got_ref[...].astype(F32)

    spec = pl.BlockSpec((rows, width), lambda i: (0, 0))
    return call(
        added_last,
        [],
        [held, got] + ([] if buffer is None else [buffer]),
        [spec, spec] + ([] if buffer is None else [ANY]),
        after,
        jax.ShapeDtypeStruct((rows, modes), F32),
        pl.BlockSpec((rows, width), lambda i: (0, at // width)),
        (1,),
        [],
        held.size,
        None if buffer is None else 0,
    )


def passed_along(block, distance):
    size = lax.axis_size("mesh")
    return lax.ppermute(block, "mesh", [((i - distance) % size, i) for i in range(size)])


def swapped(block, bit):
    size = lax.axis_size("mesh")
    return lax.ppermute(block, "mesh", [(i, i ^ (1 << bit)) for i in range(size)])


def halving_order(size):
    bits = list(range(size.bit_length() - 1))
    return [0, 2, 1] + bits[3:] if len(bits) > 2 else bits


def planned(levels):
    steps, arrived, before = [], 4.0, 4.0
    for j, eighths in enumerate(EIGHTHS):
        size = eighths / 2
        arrived += 20.0 * size
        steps.append((before - 6.0 if j else 0.0, "far", j))
        steps.append((before - 3.0 if j else 0.0, "near", j))
        steps.append((arrived, "panel", j))
        at = arrived + 4.0 + 5.0 * size
        for level in range(1, levels):
            steps.append((at, level, j))
            at += (2.0 + 12.0 * size) if level == 1 else (2.0 + 7.0 * size)
        steps.append((at, levels, j))
        before = arrived
    return [step[1:] for step in sorted(steps, key=lambda step: step[0])]


def per_device(struct_modes, acoustic_modes, coupling, face_shift, face_blocks):
    size = lax.axis_size("mesh")
    me = lax.axis_index("mesh")
    modes = acoustic_modes.shape[1]
    share = struct_modes.shape[1] // size
    order = halving_order(size)
    levels = len(order)
    widths = [e * modes // 8 for e in EIGHTHS]
    starts = [sum(widths[:j]) for j in range(len(widths))]

    state = [dict(bits=sorted(order[1:], reverse=True)) for _ in widths]
    token, buffer, lefts = [], None, None
    for stage, j in planned(levels):
        now = state[j]
        if stage in ("far", "near"):
            classes = (0, 4) if stage == "far" else (1, 3, 2)
            made = coupled(
                face_blocks, acoustic_modes, coupling, classes, starts[j], widths[j], token
            )
            for k, block in zip(classes, made):
                now[k] = block if k == 2 else passed_along(block, 2 - k)
            token = [made[0]]
            if stage == "near" and lefts is None:
                lefts = turned(me & 1, struct_modes, share, token)
                token = [lefts[0]]
        elif stage == "panel":
            pieces = [now[k] for k in range(CLASSES)]
            away, picked = panel_sent(face_shift, lefts[1], pieces, token)
            now["got"] = swapped(away, order[0])
            now["held"] = panel_kept(lefts[0], picked, [])
            token = [now["held"]]
        elif stage < levels:
            bit = order[stage]
            place = now["bits"].index(bit)
            now["bits"].remove(bit)
            now["held"], away = added(
                now["held"], now["got"], (me >> bit) & 1, 2**place, BF16 if stage < 4 else F32, token
            )
            now["got"] = swapped(away, bit)
            token = [now["held"]]
        else:
            token = [t for t in token if t is not buffer]
            buffer = finished(now["held"], now["got"], buffer, starts[j], modes, token)
            token = [buffer]
    return buffer


def solution(mesh):
    placed = (
        P(("member", "mesh"), None),
        P(("member", "mesh"), None),
        P("mesh", None, None),
        P("mesh"),
        P("mesh", None),
    )
    return jax.shard_map(
        per_device,
        mesh=mesh,
        in_specs=placed,
        out_specs=P(("member", "mesh"), None),
        check_vma=False,
    )
```

```python
import jax
import jax.numpy as jnp
from jax import lax
from jax.experimental import pallas as pl
from jax.experimental.pallas import tpu as pltpu
from jax.sharding import PartitionSpec as P

CLASSES = 5
EIGHTHS = (2, 2, 2, 1, 1)
LIMIT = 20 * 2**20
ANY = pl.BlockSpec(memory_space=pl.ANY)
BF16, F32 = jnp.bfloat16, jnp.float32
NEXT = ((0, 0), (1, 0), (1, 1))
BEFORE = ((0, 3), (0, 4), (1, 4))
HERE = ((0, 1), (0, 2), (1, 2), (1, 3))
FOUND = ((0, 2, 7, 9, 4), (1, 6, 8, 3, 5))


def call(body, scalars, arrays, specs, after, out_shape, out_specs, grid, scratch, alias=None):
    lead = len(scalars) + len(arrays)
    extra = len(after)
    outs = len(out_shape)

    def kernel(*refs):
        rest = refs[lead + extra :]
        body(*refs[:lead], *rest[:outs], *rest[outs + 1 :])

    return pl.pallas_call(
        kernel,
        out_shape=[*out_shape, jax.ShapeDtypeStruct((8, 128), F32)],
        grid_spec=pltpu.PrefetchScalarGridSpec(
            num_scalar_prefetch=len(scalars),
            grid=grid,
            in_specs=specs + [ANY] * extra,
            out_specs=[*out_specs, ANY],
            scratch_shapes=scratch,
        ),
        input_output_aliases={} if alias is None else {lead - 1: alias},
        compiler_params=pltpu.CompilerParams(vmem_limit_bytes=LIMIT),
        cost_estimate=pl.CostEstimate(flops=0, bytes_accessed=0, transcendentals=0),
        name=body.__name__,
    )(*scalars, *arrays, *after)


def halved(core, acoustic, after):
    rows, modes = acoustic.shape
    tile = modes // 4

    def other_half(core_ref, in_ref, out_ref):
        out_ref[...] = in_ref[...]

    return call(
        other_half,
        [core],
        [acoustic],
        [pl.BlockSpec((rows, tile), lambda i, c: (0, 2 * (1 - c[0]) + i))],
        after,
        [jax.ShapeDtypeStruct((rows, modes // 2), BF16)],
        [pl.BlockSpec((rows, tile), lambda i, c: (0, i))],
        (2,),
        [],
    )


def coupled(core, blocks, acoustic, coupling, at, width, after):
    slots, rows, depth = coupling[0].shape
    per = slots // CLASSES
    nodes, modes = acoustic[0].shape
    steps = modes // 2 // width
    lists = (NEXT, BEFORE, HERE)

    def coupled_rows(core_ref, own_blocks, far_blocks, own_a, far_a, own_c, far_c, *refs):
        outs, both, picked = refs[:3], refs[3], refs[4]
        core = core_ref[0]
        both[pl.ds(pl.multiple_of(core * nodes, nodes), nodes), :] = own_a[...]
        both[pl.ds(pl.multiple_of((1 - core) * nodes, nodes), nodes), :] = far_a[...]
        for out, pairs in zip(outs, lists):
            for place, (face, k) in enumerate(pairs):
                own = core == face
                for s in range(per):
                    slot = k * per + s
                    for n in range(depth // rows):
                        block = jnp.where(own, own_blocks[slot, n], far_blocks[slot, n])
                        first = pl.multiple_of(face * nodes + block * rows, rows)
                        picked[n * rows : (n + 1) * rows, :] = both[pl.ds(first, rows), :]
                    weights = jnp.where(own, own_c[slot], far_c[slot])
                    row = (place * per + s) * rows
                    out[row : row + rows, :] = jnp.dot(
                        weights, picked[...], preferred_element_type=F32
                    ).astype(BF16)

    shapes = [(len(pairs) * per * rows, width) for pairs in lists]
    return call(
        coupled_rows,
        [core, *blocks],
        [*acoustic, *coupling],
        [
            pl.BlockSpec((nodes, width), lambda i, c, *_: (0, c[0] * steps + at // width)),
            pl.BlockSpec((nodes, width), lambda i, *_: (0, at // width)),
        ]
        + [pl.BlockSpec(coupling[0].shape, lambda i, *_: (0, 0, 0))] * 2,
        after,
        [jax.ShapeDtypeStruct(shape, BF16) for shape in shapes],
        [pl.BlockSpec(shape, lambda i, *_: (0, 0)) for shape in shapes],
        (1,),
        [pltpu.VMEM((2 * nodes, width), BF16), pltpu.VMEM((depth, width), BF16)],
    )


def turned(side, bit, struct_modes, share, after):
    depth, modes = struct_modes.shape
    half = modes // 2
    low = 2**bit

    def turn(side_ref, kept_ref, sent_ref, kept_out, sent_out):
        kept_out[...] = kept_ref[...].T
        sent_out[...] = sent_ref[...].T

    if share % 128:
        sides = struct_modes.T.reshape(-1, 2, low * share, depth)
        pair = [
            lax.dynamic_index_in_dim(sides, one, 1, keepdims=False).reshape(half, depth)
            for one in (side[0], 1 - side[0])
        ]
        return [*pair, after[0]]

    def column(i, which):
        return (0, i // low * 2 * low + which * low + i % low)

    return call(
        turn,
        [side],
        [struct_modes, struct_modes],
        [
            pl.BlockSpec((depth, share), lambda i, s: column(i, s[0])),
            pl.BlockSpec((depth, share), lambda i, s: column(i, 1 - s[0])),
        ],
        after,
        [jax.ShapeDtypeStruct((half, depth), BF16)] * 2,
        [pl.BlockSpec((share, depth), lambda i, s: (i, 0))] * 2,
        (half // share,),
        [],
    )


def panel(core, shifts, lefts, pieces, after):
    (kept, sent), (far_kept, far_sent) = lefts
    tall, depth = kept.shape
    width = pieces[0].shape[1]
    tile = min(tall, 256)
    steps = tall // tile
    count = shifts[0].shape[0]
    rows = depth // count
    per = pieces[0].shape[0] // len(NEXT) // rows

    def panel_part(core_ref, own_shift, far_shift, own_k, own_s, far_k, far_s, *refs):
        parts, kept_ref, sent_ref, picked = refs[:3], refs[3], refs[4], refs[5]
        step = pl.program_id(0)

        @pl.when(step == 0)
        def _():
            for half, shift in enumerate((own_shift, far_shift)):
                first_core = core_ref[0] == half
                seen = [jnp.int32(0)] * CLASSES
                for b in range(count):
                    kind = shift[b]
                    slot = jnp.int32(0)
                    for k in range(CLASSES):
                        group = jnp.where(first_core, FOUND[0][k], FOUND[1][k])
                        slot = jnp.where(kind == k, group * per + seen[k], slot)
                        seen[k] = seen[k] + (kind == k).astype(jnp.int32)
                    row = (half * count + b) * rows
                    base = 0
                    for part in parts:
                        many = part.shape[0] // rows

                        @pl.when((slot >= base) & (slot < base + many))
                        def _(part=part, row=row, slot=slot, base=base):
                            first = pl.multiple_of((slot - base) * rows, rows)
                            picked[row : row + rows, :] = part[pl.ds(first, rows), :]

                        base += many

        def product(own, far):
            return jnp.dot(own[...], picked[:depth, :], preferred_element_type=F32) + jnp.dot(
                far[...], picked[depth:, :], preferred_element_type=F32
            )

        @pl.when(step < steps)
        def _():
            sent_ref[...] = product(own_s, far_s).astype(BF16)

        @pl.when(step >= steps)
        def _():
            kept_ref[...] = product(own_k, far_k)

    early = lambda i, *_: (jnp.minimum(i, steps - 1), 0)
    late = lambda i, *_: (jnp.maximum(i - steps, 0), 0)
    return call(
        panel_part,
        [core, *shifts],
        [kept, sent, far_kept, far_sent, *pieces],
        [
            pl.BlockSpec((tile, depth), late),
            pl.BlockSpec((tile, depth), early),
            pl.BlockSpec((tile, depth), late),
            pl.BlockSpec((tile, depth), early),
        ]
        + [pl.BlockSpec(piece.shape, lambda i, *_: (0, 0)) for piece in pieces],
        after,
        [jax.ShapeDtypeStruct((tall, width), F32), jax.ShapeDtypeStruct((tall, width), BF16)],
        [pl.BlockSpec((tile, width), late), pl.BlockSpec((tile, width), early)],
        (2 * steps,),
        [pltpu.VMEM((2 * depth, width), BF16)],
    )


def added(held, got, here, before, wire, after):
    width = held.shape[1]
    shape = (before, 2, held.shape[0] // before // 2, width)
    block = (1, *shape[1:])
    out = (shape[0] * shape[2], width)

    def added_split(here_ref, held_ref, got_ref, kept_ref, away_ref):
        side = here_ref[0]
        kept_ref[...] = held_ref[0, side] + got_ref[0, side].astype(F32)
        away_ref[...] = (held_ref[0, 1 - side] + got_ref[0, 1 - side].astype(F32)).astype(wire)

    return call(
        added_split,
        [here],
        [held.reshape(shape), got.reshape(shape)],
        [pl.BlockSpec(block, lambda i, h: (i, 0, 0, 0))] * 2,
        after,
        [jax.ShapeDtypeStruct(out, F32), jax.ShapeDtypeStruct(out, wire)],
        [pl.BlockSpec(shape[2:], lambda i, h: (i, 0))] * 2,
        (before,),
        [],
    )


def placed_in(core, block, buffer, half, at, modes, after):
    rows, width = block.shape
    steps = modes // 2 // width

    def place(core_ref, block_ref, *refs):
        refs[-1][...] = block_ref[...]

    def column(i, c):
        return (0, (c[0] if half == 0 else 1 - c[0]) * steps + at // width)

    return call(
        place,
        [core],
        [block] + ([] if buffer is None else [buffer]),
        [pl.BlockSpec((rows, width), lambda i, c: (0, 0))] + ([] if buffer is None else [ANY]),
        after,
        [jax.ShapeDtypeStruct((rows, modes), F32)],
        [pl.BlockSpec((rows, width), column)],
        (1,),
        [],
        None if buffer is None else 0,
    )


def passed_along(block, distance):
    size = lax.axis_size("mesh")
    return lax.ppermute(block, "mesh", [((i - distance) % size, i) for i in range(size)])


def swapped(block, bit):
    size = lax.axis_size("mesh")
    return lax.ppermute(block, "mesh", [(i, i ^ (1 << bit)) for i in range(size)])


def planned(levels):
    steps, arrived, before = [], 10.0, 10.0
    for j, eighths in enumerate(EIGHTHS):
        size = eighths / 2
        arrived += 20.0 * size
        steps.append((before - 4.0 if j else 0.0, "coupled", j))
        steps.append((arrived, "panel", j))
        at = arrived + 4.0
        for level in range(1, levels + 1):
            at += (2.0 + 12.0 * size) if level == 1 else (2.0 + 7.0 * size)
            steps.append((at, level, j))
        steps.append((at + 5.0, "last", j))
        before = arrived
    return [step[1:] for step in sorted(steps, key=lambda step: step[0])]


def per_device(struct_modes, acoustic_modes, coupling, face_shift, face_blocks):
    size = lax.axis_size("mesh")
    me = lax.axis_index("mesh")
    modes = acoustic_modes.shape[1]
    share = struct_modes.shape[1] // size
    bits = list(range(1, size.bit_length() - 1))
    order = [2, 1, *bits[2:]]
    levels = len(order)
    widths = [e * modes // 16 for e in EIGHTHS]
    starts = [sum(widths[:j]) for j in range(len(widths))]

    def bit_of(bit):
        return ((me >> bit) & 1).reshape(1)

    core = bit_of(0)
    half, token = halved(core, acoustic_modes, [])
    token = [token]
    blocks = (face_blocks, swapped(face_blocks, 0))
    couplings = (coupling, swapped(coupling, 0))
    acoustics = (acoustic_modes, swapped(half, 0))
    far_struct = swapped(struct_modes, 0)
    shifts = (face_shift, swapped(face_shift, 0))
    *own, last = turned(bit_of(order[0]), order[0], struct_modes, share, token)
    lefts, token = [own], [last]

    state = [dict(bits=sorted([0, *order[1:]], reverse=True)) for _ in widths]
    buffer = None
    for stage, j in planned(levels):
        now = state[j]
        if stage == "coupled":
            ahead, behind, here, last = coupled(
                core, blocks, acoustics, couplings, starts[j], widths[j], token
            )
            now["pieces"] = [passed_along(ahead, 2), passed_along(behind, -2), here]
            token = [last]
            if len(lefts) == 1:
                *far, last = turned(bit_of(order[0]), order[0], far_struct, share, token)
                lefts.append(far)
                token = [last]
        elif stage == "panel":
            now["held"], away, last = panel(core, shifts, lefts, now["pieces"], token)
            now["got"] = swapped(away, order[0])
            token = [last]
        elif stage == "last":
            buffer, last = placed_in(core, now["held"], buffer, 0, starts[j], modes, token)
            buffer, last = placed_in(core, now["got"], buffer, 1, starts[j], modes, [last])
            token = [last]
        else:
            bit = order[stage] if stage < levels else 0
            place = now["bits"].index(bit)
            now["bits"].remove(bit)
            wire = BF16 if stage < min(levels, 3) else F32
            now["held"], away, last = added(
                now["held"], now["got"], bit_of(bit), 2**place, wire, token
            )
            now["got"] = swapped(away, bit)
            token = [last]
    return buffer


def solution(mesh):
    placed = (
        P(("member", "mesh"), None),
        P(("member", "mesh"), None),
        P("mesh", None, None),
        P("mesh"),
        P("mesh", None),
    )
    return jax.shard_map(
        per_device,
        mesh=mesh,
        in_specs=placed,
        out_specs=P(("member", "mesh"), None),
        check_vma=False,
    )
```

```python
import jax
import jax.numpy as jnp
from jax import lax
from jax.experimental import pallas as pl
from jax.experimental.pallas import tpu as pltpu
from jax.sharding import PartitionSpec as P

CLASSES = 5
UNITS = (3, 3, 2)
LIMIT = 16 * 2**20
COVER = 10**11
ANY = pl.BlockSpec(memory_space=pl.ANY)
BF16, F32 = jnp.bfloat16, jnp.float32
NEXT = ((0, 0), (1, 0), (1, 1))
BEFORE = ((0, 3), (0, 4), (1, 4))
HERE = ((0, 1), (0, 2), (1, 2), (1, 3))
FOUND = ((0, 2, 7, 9, 4), (1, 6, 8, 3, 5))


def call(body, scalars, arrays, after, out_shape, scratch=(), flops=10**11):
    lead = len(scalars) + len(arrays)
    extra = len(after)
    outs = len(out_shape)

    def kernel(*refs):
        rest = refs[lead + extra :]
        body(*refs[:lead], *rest[:outs], *rest[outs + 1 :])

    kernel.__name__ = body.__name__
    vmem = pl.BlockSpec(memory_space=pltpu.VMEM)
    return pl.pallas_call(
        kernel,
        out_shape=[*out_shape, jax.ShapeDtypeStruct((8, 128), F32)],
        in_specs=[pl.BlockSpec(memory_space=pltpu.SMEM)] * len(scalars) + [vmem] * len(arrays) + [ANY] * extra,
        out_specs=[vmem] * outs + [ANY],
        scratch_shapes=scratch,
        compiler_params=pltpu.CompilerParams(vmem_limit_bytes=LIMIT),
        cost_estimate=pl.CostEstimate(flops=flops, bytes_accessed=1, transcendentals=0),
        name=body.__name__,
    )(*scalars, *arrays, *after)


def coupled(core, blocks, acoustic, coupling, at, width, after):
    slots, rows, depth = coupling[0].shape
    per = slots // CLASSES
    nodes, modes = acoustic[0].shape
    lists = (NEXT, BEFORE, HERE)

    def coupled_rows(core_ref, own_blocks, far_blocks, own_a, far_a, own_c, far_c, *refs):
        outs, both, picked = refs[:3], refs[3], refs[4]
        core = core_ref[0]
        columns = pl.ds(pl.multiple_of(core * (modes // 2) + at, 128), width)
        both[pl.ds(pl.multiple_of(core * nodes, nodes), nodes), :] = own_a[:, columns]
        both[pl.ds(pl.multiple_of((1 - core) * nodes, nodes), nodes), :] = far_a[:, columns]
        for out, pairs in zip(outs, lists):
            for place, (face, k) in enumerate(pairs):
                own = core == face
                for s in range(per):
                    slot = k * per + s
                    for n in range(depth // rows):
                        block = jnp.where(own, own_blocks[slot, n], far_blocks[slot, n])
                        first = pl.multiple_of(face * nodes + block * rows, rows)
                        picked[n * rows : (n + 1) * rows, :] = both[pl.ds(first, rows), :]
                    weights = jnp.where(own, own_c[slot], far_c[slot])
                    row = (place * per + s) * rows
                    out[row : row + rows, :] = jnp.dot(
                        weights, picked[...], preferred_element_type=F32
                    ).astype(BF16)

    shapes = [(len(pairs) * per * rows, width) for pairs in lists]
    return call(
        coupled_rows,
        [core, *blocks],
        [*acoustic, *coupling],
        after,
        [jax.ShapeDtypeStruct(shape, BF16) for shape in shapes],
        [pltpu.VMEM((2 * nodes, width), BF16), pltpu.VMEM((depth, width), BF16)],
    )


def turned(side, bit, struct_modes, share, after):
    depth, modes = struct_modes.shape
    half = modes // 2
    low = 2**bit

    def turn(side_ref, in_ref, kept_out, sent_out):
        for which, out in ((side_ref[0], kept_out), (1 - side_ref[0], sent_out)):
            for i in range(half // share):
                column = (i // low * 2 * low + i % low + which * low) * share
                block = in_ref[:, pl.ds(pl.multiple_of(column, share), share)]
                out[i * share : (i + 1) * share, :] = block.T

    if share % 128:
        sides = struct_modes.T.reshape(-1, 2, low * share, depth)
        pair = [
            lax.dynamic_index_in_dim(sides, one, 1, keepdims=False).reshape(half, depth)
            for one in (side[0], 1 - side[0])
        ]
        return [*pair, after[0]]
    return call(turn, [side], [struct_modes], after, [jax.ShapeDtypeStruct((half, depth), BF16)] * 2)


def rows_times(left_own, left_far, picked, out):
    tall, depth = left_own.shape
    tile = min(tall, 256)

    @pl.loop(0, tall // tile)
    def _(i):
        here = pl.ds(pl.multiple_of(i * tile, tile), tile)
        product = jnp.dot(left_own[here, :], picked[:depth, :], preferred_element_type=F32)
        product += jnp.dot(left_far[here, :], picked[depth:, :], preferred_element_type=F32)
        out[here, :] = product.astype(out.dtype)


def panel_sent(core, shifts, lefts, pieces, after):
    tall, depth = lefts[0].shape
    width = pieces[0].shape[1]
    count = shifts[0].shape[0]
    rows = depth // count
    per = pieces[0].shape[0] // len(NEXT) // rows

    def panel_away(core_ref, own_shift, far_shift, own, far, *refs):
        parts, sent, picked = refs[:3], refs[3], refs[4]
        for half, shift in enumerate((own_shift, far_shift)):
            first_core = core_ref[0] == half
            seen = [jnp.int32(0)] * CLASSES
            for b in range(count):
                kind = shift[b]
                slot = jnp.int32(0)
                for k in range(CLASSES):
                    group = jnp.where(first_core, FOUND[0][k], FOUND[1][k])
                    slot = jnp.where(kind == k, group * per + seen[k], slot)
                    seen[k] = seen[k] + (kind == k).astype(jnp.int32)
                row = (half * count + b) * rows
                base = 0
                for part in parts:
                    many = part.shape[0] // rows

                    @pl.when((slot >= base) & (slot < base + many))
                    def _(part=part, row=row, slot=slot, base=base):
                        first = pl.multiple_of((slot - base) * rows, rows)
                        picked[row : row + rows, :] = part[pl.ds(first, rows), :]

                    base += many
        rows_times(own, far, picked, sent)

    return call(
        panel_away,
        [core, *shifts],
        [*lefts, *pieces],
        after,
        [jax.ShapeDtypeStruct((tall, width), BF16), jax.ShapeDtypeStruct((2 * depth, width), BF16)],
        flops=COVER,
    )


def panel_kept(lefts, picked, after):
    def panel_own(own, far, picked_ref, kept):
        rows_times(own, far, picked_ref, kept)

    shape = (lefts[0].shape[0], picked.shape[1])
    return call(panel_own, [], [*lefts, picked], after, [jax.ShapeDtypeStruct(shape, F32)])


def added(held, got, here, before, wire, after):
    width = held.shape[1]
    shape = (before, 2, held.shape[0] // before // 2, width)
    tall = shape[2]

    def added_split(here_ref, held_ref, got_ref, kept_ref, away_ref):
        side = here_ref[0]
        for i in range(before):
            at = slice(i * tall, (i + 1) * tall)
            kept_ref[at, :] = held_ref[i, side] + got_ref[i, side].astype(F32)
            away_ref[at, :] = (held_ref[i, 1 - side] + got_ref[i, 1 - side].astype(F32)).astype(wire)

    out = (before * tall, width)
    return call(
        added_split,
        [here],
        [held.reshape(shape), got.reshape(shape)],
        after,
        [jax.ShapeDtypeStruct(out, F32), jax.ShapeDtypeStruct(out, wire)],
    )


def together(core, own, far, starts, modes):
    rows = own[0].shape[0]

    def put_together(core_ref, *refs):
        out = refs[-1]
        for half, blocks in enumerate((refs[: len(own)], refs[len(own) : -1])):
            side = core_ref[0] if half == 0 else 1 - core_ref[0]
            for at, block in zip(starts, blocks):
                first = pl.multiple_of(side * (modes // 2) + at, 128)
                out[:, pl.ds(first, block.shape[1])] = block[...]

    out, _ = call(put_together, [core], [*own, *far], [], [jax.ShapeDtypeStruct((rows, modes), F32)])
    return out


def passed_along(block, distance):
    size = lax.axis_size("mesh")
    return lax.ppermute(block, "mesh", [((i - distance) % size, i) for i in range(size)])


def swapped(block, bit):
    size = lax.axis_size("mesh")
    return lax.ppermute(block, "mesh", [(i, i ^ (1 << bit)) for i in range(size)])


def planned(levels):
    steps, arrived, issued = [], 10.0, [0.0, 0.0]
    for j, units in enumerate(UNITS):
        size = units / 2
        arrived += 20.0 * size
        steps.append((max(issued[j] - 4.0, 0.0), "coupled", j))
        steps.append((arrived, "panel", j))
        at = arrived + 4.0
        for level in range(1, levels + 1):
            at += (2.0 + 12.0 * size) if level == 1 else (2.0 + 7.0 * size)
            steps.append((at, level, j))
        issued.append(arrived)
    return [step[1:] for step in sorted(steps, key=lambda step: step[0])]


def per_device(struct_modes, acoustic_modes, coupling, face_shift, face_blocks):
    size = lax.axis_size("mesh")
    me = lax.axis_index("mesh")
    modes = acoustic_modes.shape[1]
    share = struct_modes.shape[1] // size
    bits = list(range(1, size.bit_length() - 1))
    order = [2, 1, *bits[2:]]
    levels = len(order)
    widths = [units * (modes // 2 // sum(UNITS)) for units in UNITS]
    starts = [sum(widths[:j]) for j in range(len(widths))]

    def bit_of(bit):
        return ((me >> bit) & 1).reshape(1)

    core = bit_of(0)
    token = []
    blocks = (face_blocks, swapped(face_blocks, 0))
    couplings = (coupling, swapped(coupling, 0))
    acoustics = (acoustic_modes, swapped(acoustic_modes, 0))
    far_struct = swapped(struct_modes, 0)
    shifts = (face_shift, swapped(face_shift, 0))
    lefts = []

    state = [dict(bits=sorted([0, *order[1:]], reverse=True)) for _ in widths]
    for stage, j in planned(levels):
        now = state[j]
        if stage == "coupled":
            ahead, behind, here, last = coupled(
                core, blocks, acoustics, couplings, starts[j], widths[j], token
            )
            now["pieces"] = [passed_along(ahead, 2), passed_along(behind, -2), here]
            token = [last]
            for one in (struct_modes, far_struct) if not lefts else ():
                *pair, last = turned(bit_of(order[0]), order[0], one, share, token)
                lefts.append(pair)
                token = [last]
        elif stage == "panel":
            kept, sent = zip(*lefts)
            away, picked, last = panel_sent(core, shifts, sent, now["pieces"], token)
            now["got"] = swapped(away, order[0])
            now["held"], last = panel_kept(kept, picked, [last])
            token = [last]
        else:
            bit = order[stage] if stage < levels else 0
            place = now["bits"].index(bit)
            now["bits"].remove(bit)
            wire = BF16 if stage < min(levels, 3) else F32
            now["held"], away, last = added(
                now["held"], now["got"], bit_of(bit), 2**place, wire, token
            )
            now["got"] = swapped(away, bit)
            token = [last]
    return together(
        core, [now["held"] for now in state], [now["got"] for now in state], starts, modes
    )


def solution(mesh):
    placed = (
        P(("member", "mesh"), None),
        P(("member", "mesh"), None),
        P("mesh", None, None),
        P("mesh"),
        P("mesh", None),
    )
    return jax.shard_map(
        per_device,
        mesh=mesh,
        in_specs=placed,
        out_specs=P(("member", "mesh"), None),
        check_vma=False,
    )
```

```python
import jax
import jax.numpy as jnp
from jax import lax
from jax.experimental import pallas as pl
from jax.experimental.pallas import tpu as pltpu
from jax.sharding import PartitionSpec as P

CLASSES = 5
UNITS = (2, 2, 2, 2)
PARTS = 2
EARLY = 4
LIMIT = 16 * 2**20
ANY = pl.BlockSpec(memory_space=pl.ANY)
BF16, F32 = jnp.bfloat16, jnp.float32
NEXT = ((0, 0), (1, 0), (1, 1))
BEFORE = ((0, 3), (0, 4), (1, 4))
HERE = ((0, 1), (0, 2), (1, 2), (1, 3))
FOUND = ((0, 2, 7, 9, 4), (1, 6, 8, 3, 5))


def call(body, scalars, arrays, after, out_shape, scratch=(), fetched=0, scalar_out=False):
    lead = len(scalars) + len(arrays)
    extra = len(after)
    outs = len(out_shape)

    def kernel(*refs):
        rest = refs[lead + extra :]
        body(*refs[:lead], *rest[:outs], *rest[outs + 1 :])

    kernel.__name__ = body.__name__
    vmem, smem = (pl.BlockSpec(memory_space=space) for space in (pltpu.VMEM, pltpu.SMEM))
    return pl.pallas_call(
        kernel,
        out_shape=[*out_shape, jax.ShapeDtypeStruct((8, 128), F32)],
        in_specs=[smem] * len(scalars)
        + ([ANY] * fetched or [vmem] * len(arrays))
        + [ANY] * extra,
        out_specs=[smem if scalar_out else vmem] * outs + [ANY],
        scratch_shapes=scratch,
        compiler_params=pltpu.CompilerParams(vmem_limit_bytes=LIMIT),
        cost_estimate=pl.CostEstimate(flops=1, bytes_accessed=1, transcendentals=0),
        name=body.__name__,
    )(*scalars, *arrays, *after)


def coupled(core, blocks, acoustic, coupling, at, width, after):
    slots, rows, depth = coupling[0].shape
    per = slots // CLASSES
    nodes, modes = acoustic[0].shape
    lists = (NEXT, BEFORE, HERE)

    def coupled_rows(core_ref, own_blocks, far_blocks, own_a, far_a, own_c, far_c, *refs):
        outs, both, weights, picked, sems = refs[:3], *refs[3:]
        core = core_ref[0]
        columns = pl.ds(pl.multiple_of(core * (modes // 2) + at, 128), width)
        copies = []
        for i, (a, c) in enumerate(((own_a, own_c), (far_a, far_c))):
            side = core if i == 0 else 1 - core
            nodes_here = pl.ds(pl.multiple_of(side * nodes, nodes), nodes)
            copies.append(pltpu.make_async_copy(a.at[:, columns], both.at[nodes_here, :], sems.at[2 * i]))
            copies.append(pltpu.make_async_copy(c, weights.at[side], sems.at[2 * i + 1]))
        for copy in copies:
            copy.start()
        for copy in copies:
            copy.wait()
        for out, pairs in zip(outs, lists):
            for place, (face, k) in enumerate(pairs):
                own = core == face
                for s in range(per):
                    slot = k * per + s
                    for n in range(depth // rows):
                        block = jnp.where(own, own_blocks[slot, n], far_blocks[slot, n])
                        first = pl.multiple_of(face * nodes + block * rows, rows)
                        picked[n * rows : (n + 1) * rows, :] = both[pl.ds(first, rows), :]
                    row = (place * per + s) * rows
                    out[row : row + rows, :] = jnp.dot(
                        weights[face, slot], picked[...], preferred_element_type=F32
                    ).astype(BF16)

    shapes = [(len(pairs) * per * rows, width) for pairs in lists]
    return call(
        coupled_rows,
        [core, *blocks],
        [*acoustic, *coupling],
        after,
        [jax.ShapeDtypeStruct(shape, BF16) for shape in shapes],
        [
            pltpu.VMEM((2 * nodes, width), BF16),
            pltpu.VMEM((2, *coupling[0].shape), BF16),
            pltpu.VMEM((depth, width), BF16),
            pltpu.SemaphoreType.DMA((4,)),
        ],
        fetched=4,
    )


def turned(side, bit, struct_modes, share, after):
    depth, modes = struct_modes.shape
    half = modes // 2
    low = 2**bit

    def turn(side_ref, in_ref, kept_out, sent_out):
        for which, out in ((side_ref[0], kept_out), (1 - side_ref[0], sent_out)):
            for i in range(half // share):
                column = (i // low * 2 * low + i % low + which * low) * share
                block = in_ref[:, pl.ds(pl.multiple_of(column, share), share)]
                out[i * share : (i + 1) * share, :] = block.T

    if share % 128:
        sides = struct_modes.T.reshape(-1, 2, low * share, depth)
        pair = [
            lax.dynamic_index_in_dim(sides, one, 1, keepdims=False).reshape(half, depth)
            for one in (side[0], 1 - side[0])
        ]
        return [*pair, after[0]]
    return call(turn, [side], [struct_modes], after, [jax.ShapeDtypeStruct((half, depth), BF16)] * 2)


def rows_times(left_own, left_far, picked, out):
    tall, depth = left_own.shape
    tile = min(tall, 256)

    @pl.loop(0, tall // tile)
    def _(i):
        here = pl.ds(pl.multiple_of(i * tile, tile), tile)
        product = jnp.dot(left_own[here, :], picked[:depth, :], preferred_element_type=F32)
        product += jnp.dot(left_far[here, :], picked[depth:, :], preferred_element_type=F32)
        out[here, :] = product.astype(out.dtype)


def slots_of(core, shifts, per, after):
    count = shifts[0].shape[0]

    def slots(core_ref, own_shift, far_shift, out):
        for half, shift in enumerate((own_shift, far_shift)):
            first_core = core_ref[0] == half
            bases = [jnp.where(first_core, FOUND[0][k], FOUND[1][k]) * per for k in range(CLASSES)]
            for b in range(count):
                kind = shift[b]
                slot = jnp.int32(0)
                for k in range(CLASSES):
                    slot = jnp.where(kind == k, bases[k], slot)
                    bases[k] = bases[k] + (kind == k).astype(jnp.int32)
                out[half * count + b] = slot

    shape = jax.ShapeDtypeStruct((2 * count,), jnp.int32)
    return call(slots, [core, *shifts], [], after, [shape], scalar_out=True)


def panel(slots, lefts, pieces, after):
    tall, depth = lefts[0].shape
    width = pieces[0].shape[1]
    count = slots.shape[0]
    rows = 2 * depth // count

    def panel_part(slot_ref, own_kept, far_kept, own_sent, far_sent, *refs):
        parts, away, kept, picked = refs[:3], refs[3 : 3 + PARTS], refs[3 + PARTS], refs[4 + PARTS]
        for b in range(count):
            slot = slot_ref[b]
            base = 0
            for part in parts:
                many = part.shape[0] // rows

                @pl.when((slot >= base) & (slot < base + many))
                def _(part=part, b=b, slot=slot, base=base):
                    first = pl.multiple_of((slot - base) * rows, rows)
                    picked[b * rows : (b + 1) * rows, :] = part[pl.ds(first, rows), :]

                base += many
        for i in range(PARTS):
            side = pl.ds(i * (tall // PARTS), tall // PARTS)
            rows_times(own_sent.at[side, :], far_sent.at[side, :], picked, away[i])
        rows_times(own_kept, far_kept, picked, kept)

    return call(
        panel_part,
        [slots],
        [*lefts, *pieces],
        after,
        [jax.ShapeDtypeStruct((tall // PARTS, width), BF16)] * PARTS
        + [jax.ShapeDtypeStruct((tall, width), F32)],
        [pltpu.VMEM((2 * depth, width), BF16)],
    )


def added(held, got, here, before, wire, after):
    width = held.shape[1]
    shape = (before, 2, held.shape[0] // before // 2, width)
    tall = shape[2]
    each = before // len(got)

    def added_split(here_ref, held_ref, *refs):
        kept_ref, away_ref = refs[-2:]
        side = here_ref[0]
        for i in range(before):
            at = slice(i * tall, (i + 1) * tall)
            arrived = refs[i // each]
            kept_ref[at, :] = held_ref[i, side] + arrived[i % each, side].astype(F32)
            away = held_ref[i, 1 - side] + arrived[i % each, 1 - side].astype(F32)
            away_ref[at, :] = away.astype(wire)

    out = (before * tall, width)
    return call(
        added_split,
        [here],
        [held.reshape(shape), *[block.reshape(each, *shape[1:]) for block in got]],
        after,
        [jax.ShapeDtypeStruct(out, F32), jax.ShapeDtypeStruct(out, wire)],
    )


def together(core, own, far, starts, modes):
    rows = own[0].shape[0]

    def put_together(core_ref, *refs):
        out = refs[-1]
        for half, blocks in enumerate((refs[: len(own)], refs[len(own) : -1])):
            side = core_ref[0] if half == 0 else 1 - core_ref[0]
            for at, block in zip(starts, blocks):
                first = pl.multiple_of(side * (modes // 2) + at, 128)
                out[:, pl.ds(first, block.shape[1])] = block[...]

    out, _ = call(put_together, [core], [*own, *far], [], [jax.ShapeDtypeStruct((rows, modes), F32)])
    return out


def passed_along(block, distance):
    size = lax.axis_size("mesh")
    return lax.ppermute(block, "mesh", [((i - distance) % size, i) for i in range(size)])


def swapped(block, bit):
    size = lax.axis_size("mesh")
    return lax.ppermute(block, "mesh", [(i, i ^ (1 << bit)) for i in range(size)])


def planned(levels):
    chunks = len(UNITS)
    steps = [("coupled", 0), ("turned", 0), *(("coupled", j) for j in range(1, EARLY))]
    for now in range(chunks + levels):
        steps.append(("panel", now))
        steps.extend((level, now - level) for level in range(1, levels + 1))
        steps.append(("coupled", now + EARLY))
    return [step for step in steps if 0 <= step[1] < chunks]


def per_device(struct_modes, acoustic_modes, coupling, face_shift, face_blocks):
    size = lax.axis_size("mesh")
    me = lax.axis_index("mesh")
    modes = acoustic_modes.shape[1]
    share = struct_modes.shape[1] // size
    bits = list(range(1, size.bit_length() - 1))
    order = [2, 1, *bits[2:]]
    levels = len(order)
    widths = [units * (modes // 2 // sum(UNITS)) for units in UNITS]
    starts = [sum(widths[:j]) for j in range(len(widths))]

    def bit_of(bit):
        return ((me >> bit) & 1).reshape(1)

    core = bit_of(0)
    token = []
    blocks = (face_blocks, swapped(face_blocks, 0))
    couplings = (coupling, swapped(coupling, 0))
    acoustics = (acoustic_modes, swapped(acoustic_modes, 0))
    far_struct = swapped(struct_modes, 0)
    shifts = (face_shift, swapped(face_shift, 0))
    per = coupling.shape[0] // CLASSES
    state = [dict(bits=sorted([0, *order[1:]], reverse=True)) for _ in widths]
    finished = []
    for stage, j in planned(levels):
        now = state[j]
        if stage == "coupled":
            ahead, behind, here, last = coupled(
                core, blocks, acoustics, couplings, starts[j], widths[j], token
            )
            now["pieces"] = [passed_along(ahead, 2), passed_along(behind, -2), here]
        elif stage == "turned":
            side = bit_of(order[0])
            *own, last = turned(side, order[0], struct_modes, share, token)
            slots, last = slots_of(core, shifts, per, [last])
            *far, last = turned(side, order[0], far_struct, share, [last])
            kept, sent = zip(own, far)
        elif stage == "panel":
            *away, now["held"], last = panel(slots, (*kept, *sent), now["pieces"], token)
            now["got"] = [swapped(one, order[0]) for one in away]
        else:
            bit = order[stage] if stage < levels else 0
            place = now["bits"].index(bit)
            now["bits"].remove(bit)
            wire = BF16 if stage < min(levels, 3) else F32
            now["held"], away, last = added(
                now["held"], now["got"], bit_of(bit), 2**place, wire, token
            )
            now["got"] = [swapped(away, bit)]
        token = [last]
    return together(
        core, [now["held"] for now in state], [now["got"][0] for now in state], starts, modes
    )


def solution(mesh):
    placed = (
        P(("member", "mesh"), None),
        P(("member", "mesh"), None),
        P("mesh", None, None),
        P("mesh"),
        P("mesh", None),
    )
    return jax.shard_map(
        per_device,
        mesh=mesh,
        in_specs=placed,
        out_specs=P(("member", "mesh"), None),
        check_vma=False,
    )
```

```python
import jax
import jax.numpy as jnp
from jax import lax
from jax.experimental import pallas as pl
from jax.experimental.pallas import tpu as pltpu
from jax.sharding import PartitionSpec as P

CLASSES = 5
UNITS = (2, 2, 2, 2)
PARTS = 2
EARLY = 4
PACE = 4 * 10**9
LIMIT = 16 * 2**20
ANY = pl.BlockSpec(memory_space=pl.ANY)
BF16, F32 = jnp.bfloat16, jnp.float32
NEXT = ((0, 0), (1, 0), (1, 1))
BEFORE = ((0, 3), (0, 4), (1, 4))
HERE = ((0, 1), (0, 2), (1, 2), (1, 3))
FOUND = ((0, 2, 7, 9, 4), (1, 6, 8, 3, 5))


def call(body, scalars, arrays, after, out_shape, scratch=(), fetched=0, scalar_out=False, time=1.0):
    lead = len(scalars) + len(arrays)
    extra = len(after)
    outs = len(out_shape)

    def kernel(*refs):
        rest = refs[lead + extra :]
        body(*refs[:lead], *rest[:outs], *rest[outs + 1 :])

    kernel.__name__ = body.__name__
    vmem, smem = (pl.BlockSpec(memory_space=space) for space in (pltpu.VMEM, pltpu.SMEM))
    return pl.pallas_call(
        kernel,
        out_shape=[*out_shape, jax.ShapeDtypeStruct((8, 128), F32)],
        in_specs=[smem] * len(scalars)
        + ([ANY] * fetched or [vmem] * len(arrays))
        + [ANY] * extra,
        out_specs=[smem if scalar_out else vmem] * outs + [ANY],
        scratch_shapes=scratch,
        compiler_params=pltpu.CompilerParams(vmem_limit_bytes=LIMIT),
        cost_estimate=pl.CostEstimate(flops=int(time * PACE), bytes_accessed=1, transcendentals=0),
        name=body.__name__,
    )(*scalars, *arrays, *after)


def in_hbm(array):
    return pltpu.with_memory_space_constraint(array, pltpu.HBM)


def coupled(core, blocks, acoustic, coupling, at, width, after):
    slots, rows, depth = coupling[0].shape
    per = slots // CLASSES
    nodes, modes = acoustic[0].shape
    lists = (NEXT, BEFORE, HERE)

    def coupled_rows(core_ref, own_blocks, far_blocks, own_a, far_a, own_c, far_c, *refs):
        outs, both, weights, picked, sems = refs[:3], *refs[3:]
        core = core_ref[0]
        columns = pl.ds(pl.multiple_of(core * (modes // 2) + at, 128), width)
        copies = []
        for i, (a, c) in enumerate(((own_a, own_c), (far_a, far_c))):
            side = core if i == 0 else 1 - core
            nodes_here = pl.ds(pl.multiple_of(side * nodes, nodes), nodes)
            copies.append(pltpu.make_async_copy(a.at[:, columns], both.at[nodes_here, :], sems.at[2 * i]))
            copies.append(pltpu.make_async_copy(c, weights.at[side], sems.at[2 * i + 1]))
        for copy in copies:
            copy.start()
        for copy in copies:
            copy.wait()
        for out, pairs in zip(outs, lists):
            for place, (face, k) in enumerate(pairs):
                own = core == face
                for s in range(per):
                    slot = k * per + s
                    for n in range(depth // rows):
                        block = jnp.where(own, own_blocks[slot, n], far_blocks[slot, n])
                        first = pl.multiple_of(face * nodes + block * rows, rows)
                        picked[n * rows : (n + 1) * rows, :] = both[pl.ds(first, rows), :]
                    row = (place * per + s) * rows
                    out[row : row + rows, :] = jnp.dot(
                        weights[face, slot], picked[...], preferred_element_type=F32
                    ).astype(BF16)

    shapes = [(len(pairs) * per * rows, width) for pairs in lists]
    return call(
        coupled_rows,
        [core, *blocks],
        [in_hbm(acoustic[0]), acoustic[1], in_hbm(coupling[0]), coupling[1]],
        after,
        [jax.ShapeDtypeStruct(shape, BF16) for shape in shapes],
        [
            pltpu.VMEM((2 * nodes, width), BF16),
            pltpu.VMEM((2, *coupling[0].shape), BF16),
            pltpu.VMEM((depth, width), BF16),
            pltpu.SemaphoreType.DMA((4,)),
        ],
        fetched=4,
        time=2.5,
    )


def turned(side, bit, struct_modes, share, after):
    depth, modes = struct_modes.shape
    half = modes // 2
    low = 2**bit

    def turn(side_ref, in_ref, kept_out, sent_out):
        for which, out in ((side_ref[0], kept_out), (1 - side_ref[0], sent_out)):
            for i in range(half // share):
                column = (i // low * 2 * low + i % low + which * low) * share
                block = in_ref[:, pl.ds(pl.multiple_of(column, share), share)]
                out[i * share : (i + 1) * share, :] = block.T

    if share % 128:
        sides = struct_modes.T.reshape(-1, 2, low * share, depth)
        pair = [
            lax.dynamic_index_in_dim(sides, one, 1, keepdims=False).reshape(half, depth)
            for one in (side[0], 1 - side[0])
        ]
        return [*pair, after[0]]
    return call(turn, [side], [struct_modes], after, [jax.ShapeDtypeStruct((half, depth), BF16)] * 2, time=2.5)


def rows_times(left_own, left_far, picked, out):
    tall, depth = left_own.shape
    tile = min(tall, 256)

    @pl.loop(0, tall // tile)
    def _(i):
        here = pl.ds(pl.multiple_of(i * tile, tile), tile)
        product = jnp.dot(left_own[here, :], picked[:depth, :], preferred_element_type=F32)
        product += jnp.dot(left_far[here, :], picked[depth:, :], preferred_element_type=F32)
        out[here, :] = product.astype(out.dtype)


def slots_of(core, shifts, per, after):
    count = shifts[0].shape[0]

    def slots(core_ref, own_shift, far_shift, out):
        for half, shift in enumerate((own_shift, far_shift)):
            first_core = core_ref[0] == half
            bases = [jnp.where(first_core, FOUND[0][k], FOUND[1][k]) * per for k in range(CLASSES)]
            for b in range(count):
                kind = shift[b]
                slot = jnp.int32(0)
                for k in range(CLASSES):
                    slot = jnp.where(kind == k, bases[k], slot)
                    bases[k] = bases[k] + (kind == k).astype(jnp.int32)
                out[half * count + b] = slot

    shape = jax.ShapeDtypeStruct((2 * count,), jnp.int32)
    return call(slots, [core, *shifts], [], after, [shape], scalar_out=True)


def panel(slots, lefts, pieces, after):
    tall, depth = lefts[0].shape
    width = pieces[0].shape[1]
    count = slots.shape[0]
    rows = 2 * depth // count

    def panel_part(slot_ref, own_kept, far_kept, own_sent, far_sent, *refs):
        parts, away, kept, picked = refs[:3], refs[3 : 3 + PARTS], refs[3 + PARTS], refs[4 + PARTS]
        for b in range(count):
            slot = slot_ref[b]
            base = 0
            for part in parts:
                many = part.shape[0] // rows

                @pl.when((slot >= base) & (slot < base + many))
                def _(part=part, b=b, slot=slot, base=base):
                    first = pl.multiple_of((slot - base) * rows, rows)
                    picked[b * rows : (b + 1) * rows, :] = part[pl.ds(first, rows), :]

                base += many
        for i in range(PARTS):
            side = pl.ds(i * (tall // PARTS), tall // PARTS)
            rows_times(own_sent.at[side, :], far_sent.at[side, :], picked, away[i])
        rows_times(own_kept, far_kept, picked, kept)

    return call(
        panel_part,
        [slots],
        [*lefts, *pieces],
        after,
        [jax.ShapeDtypeStruct((tall // PARTS, width), BF16)] * PARTS
        + [jax.ShapeDtypeStruct((tall, width), F32)],
        [pltpu.VMEM((2 * depth, width), BF16)],
        time=4.0,
    )


def added(held, got, here, before, wire, after):
    width = held.shape[1]
    shape = (before, 2, held.shape[0] // before // 2, width)
    tall = shape[2]
    each = before // len(got)

    def added_split(here_ref, held_ref, *refs):
        kept_ref, away_ref = refs[-2:]
        side = here_ref[0]
        for i in range(before):
            at = slice(i * tall, (i + 1) * tall)
            arrived = refs[i // each]
            kept_ref[at, :] = held_ref[i, side] + arrived[i % each, side].astype(F32)
            away = held_ref[i, 1 - side] + arrived[i % each, 1 - side].astype(F32)
            away_ref[at, :] = away.astype(wire)

    out = (before * tall, width)
    return call(
        added_split,
        [here],
        [held.reshape(shape), *[block.reshape(each, *shape[1:]) for block in got]],
        after,
        [jax.ShapeDtypeStruct(out, F32), jax.ShapeDtypeStruct(out, wire)],
    )


def together(core, own, far, starts, modes):
    rows = own[0].shape[0]

    def put_together(core_ref, *refs):
        out = refs[-1]
        for half, blocks in enumerate((refs[: len(own)], refs[len(own) : -1])):
            side = core_ref[0] if half == 0 else 1 - core_ref[0]
            for at, block in zip(starts, blocks):
                first = pl.multiple_of(side * (modes // 2) + at, 128)
                out[:, pl.ds(first, block.shape[1])] = block[...]

    out, _ = call(put_together, [core], [*own, *far], [], [jax.ShapeDtypeStruct((rows, modes), F32)])
    return out


def passed_along(block, distance):
    size = lax.axis_size("mesh")
    return lax.ppermute(block, "mesh", [((i - distance) % size, i) for i in range(size)])


def swapped(block, bit):
    size = lax.axis_size("mesh")
    return lax.ppermute(block, "mesh", [(i, i ^ (1 << bit)) for i in range(size)])


def planned(levels):
    chunks = len(UNITS)
    steps = [("coupled", 0), ("turned", 0), *(("coupled", j) for j in range(1, EARLY))]
    for now in range(chunks + levels):
        steps.append(("panel", now))
        steps.extend((level, now - level) for level in range(1, levels + 1))
        steps.append(("coupled", now + EARLY))
    return [step for step in steps if 0 <= step[1] < chunks]


def per_device(struct_modes, acoustic_modes, coupling, face_shift, face_blocks):
    size = lax.axis_size("mesh")
    me = lax.axis_index("mesh")
    modes = acoustic_modes.shape[1]
    share = struct_modes.shape[1] // size
    bits = list(range(1, size.bit_length() - 1))
    order = [2, 1, *bits[2:]]
    levels = len(order)
    widths = [units * (modes // 2 // sum(UNITS)) for units in UNITS]
    starts = [sum(widths[:j]) for j in range(len(widths))]

    def bit_of(bit):
        return ((me >> bit) & 1).reshape(1)

    core = bit_of(0)
    token = []
    blocks = (face_blocks, swapped(face_blocks, 0))
    couplings = (coupling, swapped(coupling, 0))
    acoustics = (acoustic_modes, swapped(acoustic_modes, 0))
    shifts = (face_shift, swapped(face_shift, 0))
    per = coupling.shape[0] // CLASSES
    state = [dict(bits=sorted([0, *order[1:]], reverse=True)) for _ in widths]
    finished = []
    for stage, j in planned(levels):
        now = state[j]
        if stage == "coupled":
            ahead, behind, here, last = coupled(
                core, blocks, acoustics, couplings, starts[j], widths[j], token
            )
            now["pieces"] = [passed_along(ahead, 2), passed_along(behind, -2), here]
            if j == 0:
                later, _ = lax.optimization_barrier((struct_modes, last))
                now["far"] = swapped(later, 0)
        elif stage == "turned":
            side = bit_of(order[0])
            *own, last = turned(side, order[0], struct_modes, share, token)
            slots, last = slots_of(core, shifts, per, [last])
            *far, last = turned(side, order[0], now["far"], share, [last])
            kept, sent = zip(own, far)
        elif stage == "panel":
            *away, now["held"], last = panel(slots, (*kept, *sent), now["pieces"], token)
            now["got"] = [swapped(one, order[0]) for one in away]
        else:
            bit = order[stage] if stage < levels else 0
            place = now["bits"].index(bit)
            now["bits"].remove(bit)
            wire = BF16 if stage < min(levels, 3) else F32
            now["held"], away, last = added(
                now["held"], now["got"], bit_of(bit), 2**place, wire, token
            )
            now["got"] = [swapped(away, bit)]
        token = [last]
    return together(
        core, [now["held"] for now in state], [now["got"][0] for now in state], starts, modes
    )


def solution(mesh):
    placed = (
        P(("member", "mesh"), None),
        P(("member", "mesh"), None),
        P("mesh", None, None),
        P("mesh"),
        P("mesh", None),
    )
    return jax.shard_map(
        per_device,
        mesh=mesh,
        in_specs=placed,
        out_specs=P(("member", "mesh"), None),
        check_vma=False,
    )
```

```python
import jax
import jax.numpy as jnp
from jax import lax
from jax.experimental import pallas as pl
from jax.experimental.pallas import tpu as pltpu
from jax.sharding import PartitionSpec as P

CLASSES = 5
UNITS = (2, 2, 2, 2)
PARTS = 2
EARLY = 4
PACE = 10**10
LIMIT = 16 * 2**20
ANY = pl.BlockSpec(memory_space=pl.ANY)
BF16, F32 = jnp.bfloat16, jnp.float32
NEXT = ((0, 0), (1, 0), (1, 1))
BEFORE = ((0, 3), (0, 4), (1, 4))
HERE = ((0, 1), (0, 2), (1, 2), (1, 3))
FOUND = ((0, 2, 7, 9, 4), (1, 6, 8, 3, 5))


def call(body, scalars, arrays, after, out_shape, scratch=(), fetched=0, scalar_out=False, time=1.0):
    lead = len(scalars) + len(arrays)
    extra = len(after)
    outs = len(out_shape)

    def kernel(*refs):
        rest = refs[lead + extra :]
        body(*refs[:lead], *rest[:outs], *rest[outs + 1 :])

    kernel.__name__ = body.__name__
    vmem, smem = (pl.BlockSpec(memory_space=space) for space in (pltpu.VMEM, pltpu.SMEM))
    return pl.pallas_call(
        kernel,
        out_shape=[*out_shape, jax.ShapeDtypeStruct((8, 128), F32)],
        in_specs=[smem] * len(scalars)
        + ([ANY] * fetched or [vmem] * len(arrays))
        + [ANY] * extra,
        out_specs=[smem if scalar_out else vmem] * outs + [ANY],
        scratch_shapes=scratch,
        compiler_params=pltpu.CompilerParams(vmem_limit_bytes=LIMIT),
        cost_estimate=pl.CostEstimate(flops=int(time * PACE), bytes_accessed=1, transcendentals=0),
        name=body.__name__,
    )(*scalars, *arrays, *after)


def in_hbm(array):
    return pltpu.with_memory_space_constraint(array, pltpu.HBM)


def coupled(core, blocks, acoustic, coupling, at, width, after):
    slots, rows, depth = coupling[0].shape
    per = slots // CLASSES
    nodes, modes = acoustic[0].shape
    lists = (NEXT, BEFORE, HERE)

    def coupled_rows(core_ref, own_blocks, far_blocks, own_a, far_a, own_c, far_c, *refs):
        outs, both, weights, picked, sems = refs[:3], *refs[3:]
        core = core_ref[0]
        columns = pl.ds(pl.multiple_of(core * (modes // 2) + at, 128), width)
        copies = []
        for i, (a, c) in enumerate(((own_a, own_c), (far_a, far_c))):
            side = core if i == 0 else 1 - core
            nodes_here = pl.ds(pl.multiple_of(side * nodes, nodes), nodes)
            copies.append(pltpu.make_async_copy(a.at[:, columns], both.at[nodes_here, :], sems.at[2 * i]))
            copies.append(pltpu.make_async_copy(c, weights.at[side], sems.at[2 * i + 1]))
        for copy in copies:
            copy.start()
        for copy in copies:
            copy.wait()
        for out, pairs in zip(outs, lists):
            for place, (face, k) in enumerate(pairs):
                own = core == face
                for s in range(per):
                    slot = k * per + s
                    for n in range(depth // rows):
                        block = jnp.where(own, own_blocks[slot, n], far_blocks[slot, n])
                        first = pl.multiple_of(face * nodes + block * rows, rows)
                        picked[n * rows : (n + 1) * rows, :] = both[pl.ds(first, rows), :]
                    row = (place * per + s) * rows
                    out[row : row + rows, :] = jnp.dot(
                        weights[face, slot], picked[...], preferred_element_type=F32
                    ).astype(BF16)

    shapes = [(len(pairs) * per * rows, width) for pairs in lists]
    return call(
        coupled_rows,
        [core, *blocks],
        [in_hbm(acoustic[0]), acoustic[1], in_hbm(coupling[0]), coupling[1]],
        after,
        [jax.ShapeDtypeStruct(shape, BF16) for shape in shapes],
        [
            pltpu.VMEM((2 * nodes, width), BF16),
            pltpu.VMEM((2, *coupling[0].shape), BF16),
            pltpu.VMEM((depth, width), BF16),
            pltpu.SemaphoreType.DMA((4,)),
        ],
        fetched=4,
        time=2.5,
    )


def turned(side, bit, struct_modes, share, after):
    depth, modes = struct_modes.shape
    half = modes // 2
    low = 2**bit

    def turn(side_ref, in_ref, kept_out, sent_out):
        for which, out in ((side_ref[0], kept_out), (1 - side_ref[0], sent_out)):
            for i in range(half // share):
                column = (i // low * 2 * low + i % low + which * low) * share
                block = in_ref[:, pl.ds(pl.multiple_of(column, share), share)]
                out[i * share : (i + 1) * share, :] = block.T

    if share % 128:
        sides = struct_modes.T.reshape(-1, 2, low * share, depth)
        pair = [
            lax.dynamic_index_in_dim(sides, one, 1, keepdims=False).reshape(half, depth)
            for one in (side[0], 1 - side[0])
        ]
        return [*pair, after[0]]
    return call(turn, [side], [struct_modes], after, [jax.ShapeDtypeStruct((half, depth), BF16)] * 2, time=2.5)


def rows_times(left_own, left_far, picked, out):
    tall, depth = left_own.shape
    tile = min(tall, 256)

    @pl.loop(0, tall // tile)
    def _(i):
        here = pl.ds(pl.multiple_of(i * tile, tile), tile)
        product = jnp.dot(left_own[here, :], picked[:depth, :], preferred_element_type=F32)
        product += jnp.dot(left_far[here, :], picked[depth:, :], preferred_element_type=F32)
        out[here, :] = product.astype(out.dtype)


def slots_of(core, shifts, per, after):
    count = shifts[0].shape[0]

    def slots(core_ref, own_shift, far_shift, out):
        for half, shift in enumerate((own_shift, far_shift)):
            first_core = core_ref[0] == half
            bases = [jnp.where(first_core, FOUND[0][k], FOUND[1][k]) * per for k in range(CLASSES)]
            for b in range(count):
                kind = shift[b]
                slot = jnp.int32(0)
                for k in range(CLASSES):
                    slot = jnp.where(kind == k, bases[k], slot)
                    bases[k] = bases[k] + (kind == k).astype(jnp.int32)
                out[half * count + b] = slot

    shape = jax.ShapeDtypeStruct((2 * count,), jnp.int32)
    return call(slots, [core, *shifts], [], after, [shape], scalar_out=True)


def panel(slots, lefts, pieces, after):
    tall, depth = lefts[0].shape
    width = pieces[0].shape[1]
    count = slots.shape[0]
    rows = 2 * depth // count

    def panel_part(slot_ref, own_kept, far_kept, own_sent, far_sent, *refs):
        parts, away, kept, picked = refs[:3], refs[3 : 3 + PARTS], refs[3 + PARTS], refs[4 + PARTS]
        for b in range(count):
            slot = slot_ref[b]
            base = 0
            for part in parts:
                many = part.shape[0] // rows

                @pl.when((slot >= base) & (slot < base + many))
                def _(part=part, b=b, slot=slot, base=base):
                    first = pl.multiple_of((slot - base) * rows, rows)
                    picked[b * rows : (b + 1) * rows, :] = part[pl.ds(first, rows), :]

                base += many
        for i in range(PARTS):
            side = pl.ds(i * (tall // PARTS), tall // PARTS)
            rows_times(own_sent.at[side, :], far_sent.at[side, :], picked, away[i])
        rows_times(own_kept, far_kept, picked, kept)

    return call(
        panel_part,
        [slots],
        [*lefts, *pieces],
        after,
        [jax.ShapeDtypeStruct((tall // PARTS, width), BF16)] * PARTS
        + [jax.ShapeDtypeStruct((tall, width), F32)],
        [pltpu.VMEM((2 * depth, width), BF16)],
        time=4.0,
    )


def added(held, got, here, before, wire, after):
    width = held.shape[1]
    shape = (before, 2, held.shape[0] // before // 2, width)
    tall = shape[2]
    each = before // len(got)

    def added_split(here_ref, held_ref, *refs):
        kept_ref, away_ref = refs[-2:]
        side = here_ref[0]
        for i in range(before):
            at = slice(i * tall, (i + 1) * tall)
            arrived = refs[i // each]
            kept_ref[at, :] = held_ref[i, side] + arrived[i % each, side].astype(F32)
            away = held_ref[i, 1 - side] + arrived[i % each, 1 - side].astype(F32)
            away_ref[at, :] = away.astype(wire)

    out = (before * tall, width)
    return call(
        added_split,
        [here],
        [held.reshape(shape), *[block.reshape(each, *shape[1:]) for block in got]],
        after,
        [jax.ShapeDtypeStruct(out, F32), jax.ShapeDtypeStruct(out, wire)],
    )


def together(core, own, far, starts, modes):
    rows = own[0].shape[0]

    def put_together(core_ref, *refs):
        out = refs[-1]
        for half, blocks in enumerate((refs[: len(own)], refs[len(own) : -1])):
            side = core_ref[0] if half == 0 else 1 - core_ref[0]
            for at, block in zip(starts, blocks):
                first = pl.multiple_of(side * (modes // 2) + at, 128)
                out[:, pl.ds(first, block.shape[1])] = block[...]

    out, _ = call(put_together, [core], [*own, *far], [], [jax.ShapeDtypeStruct((rows, modes), F32)])
    return out


def passed_along(block, distance):
    size = lax.axis_size("mesh")
    return lax.ppermute(block, "mesh", [((i - distance) % size, i) for i in range(size)])


def swapped(block, bit):
    size = lax.axis_size("mesh")
    return lax.ppermute(block, "mesh", [(i, i ^ (1 << bit)) for i in range(size)])


def planned(levels):
    chunks = len(UNITS)
    steps = [("coupled", 0), ("turned", 0), *(("coupled", j) for j in range(1, EARLY))]
    for now in range(chunks + levels):
        steps.append(("panel", now))
        steps.extend((level, now - level) for level in range(1, levels + 1))
        steps.append(("coupled", now + EARLY))
    return [step for step in steps if 0 <= step[1] < chunks]


def per_device(struct_modes, acoustic_modes, coupling, face_shift, face_blocks):
    size = lax.axis_size("mesh")
    me = lax.axis_index("mesh")
    modes = acoustic_modes.shape[1]
    share = struct_modes.shape[1] // size
    bits = list(range(1, size.bit_length() - 1))
    order = [2, 1, *bits[2:]]
    levels = len(order)
    widths = [units * (modes // 2 // sum(UNITS)) for units in UNITS]
    starts = [sum(widths[:j]) for j in range(len(widths))]

    def bit_of(bit):
        return ((me >> bit) & 1).reshape(1)

    core = bit_of(0)
    token = []
    blocks = (face_blocks, swapped(face_blocks, 0))
    couplings = (coupling, swapped(coupling, 0))
    acoustics = (acoustic_modes, swapped(acoustic_modes, 0))
    shifts = (face_shift, swapped(face_shift, 0))
    per = coupling.shape[0] // CLASSES
    state = [dict(bits=sorted([0, *order[1:]], reverse=True)) for _ in widths]
    finished = []
    for stage, j in planned(levels):
        now = state[j]
        if stage == "coupled":
            ahead, behind, here, last = coupled(
                core, blocks, acoustics, couplings, starts[j], widths[j], token
            )
            now["pieces"] = [passed_along(ahead, 2), passed_along(behind, -2), here]
            if j == 0:
                later, _ = lax.optimization_barrier((struct_modes, last))
                now["far"] = swapped(later, 0)
        elif stage == "turned":
            side = bit_of(order[0])
            *own, last = turned(side, order[0], struct_modes, share, token)
            slots, last = slots_of(core, shifts, per, [last])
            *far, last = turned(side, order[0], now["far"], share, [last])
            kept, sent = zip(own, far)
        elif stage == "panel":
            *away, now["held"], last = panel(slots, (*kept, *sent), now["pieces"], token)
            now["got"] = [swapped(one, order[0]) for one in away]
        else:
            bit = order[stage] if stage < levels else 0
            place = now["bits"].index(bit)
            now["bits"].remove(bit)
            wire = BF16 if stage < min(levels, 3) else F32
            now["held"], away, last = added(
                now["held"], now["got"], bit_of(bit), 2**place, wire, token
            )
            now["got"] = [swapped(away, bit)]
        token = [last]
    return together(
        core, [now["held"] for now in state], [now["got"][0] for now in state], starts, modes
    )


def solution(mesh):
    placed = (
        P(("member", "mesh"), None),
        P(("member", "mesh"), None),
        P("mesh", None, None),
        P("mesh"),
        P("mesh", None),
    )
    return jax.shard_map(
        per_device,
        mesh=mesh,
        in_specs=placed,
        out_specs=P(("member", "mesh"), None),
        check_vma=False,
    )
```

```python
import jax
import jax.numpy as jnp
from jax import lax
from jax.experimental import pallas as pl
from jax.experimental.pallas import tpu as pltpu
from jax.sharding import PartitionSpec as P

CLASSES = 5
UNITS = (2, 2, 3, 1)
EARLY = 4
ORDERS = {3: [1, 2, 3]}
PACE = 10**10
LIMIT = 16 * 2**20
ANY = pl.BlockSpec(memory_space=pl.ANY)
BF16, F32 = jnp.bfloat16, jnp.float32
NEXT = ((0, 0), (1, 0), (1, 1))
BEFORE = ((0, 3), (0, 4), (1, 4))
HERE = ((0, 1), (0, 2), (1, 2), (1, 3))
FOUND = ((0, 2, 7, 9, 4), (1, 6, 8, 3, 5))


def call(body, scalars, arrays, after, out_shape, scratch=(), fetched=0, scalar_out=False, time=1.0):
    lead = len(scalars) + len(arrays)
    extra = len(after)
    outs = len(out_shape)

    def kernel(*refs):
        rest = refs[lead + extra :]
        body(*refs[:lead], *rest[:outs], *rest[outs + 1 :])

    kernel.__name__ = body.__name__
    vmem, smem = (pl.BlockSpec(memory_space=space) for space in (pltpu.VMEM, pltpu.SMEM))
    return pl.pallas_call(
        kernel,
        out_shape=[*out_shape, jax.ShapeDtypeStruct((8, 128), F32)],
        in_specs=[smem] * len(scalars)
        + ([ANY] * fetched or [vmem] * len(arrays))
        + [ANY] * extra,
        out_specs=[smem if scalar_out else vmem] * outs + [ANY],
        scratch_shapes=scratch,
        compiler_params=pltpu.CompilerParams(vmem_limit_bytes=LIMIT),
        cost_estimate=pl.CostEstimate(flops=int(time * PACE), bytes_accessed=1, transcendentals=0),
        name=body.__name__,
    )(*scalars, *arrays, *after)


def in_hbm(array):
    return pltpu.with_memory_space_constraint(array, pltpu.HBM)


def coupled(core, blocks, acoustic, coupling, at, width, after):
    slots, rows, depth = coupling[0].shape
    per = slots // CLASSES
    nodes, modes = acoustic[0].shape
    lists = (NEXT, BEFORE, HERE)

    def coupled_rows(core_ref, own_blocks, far_blocks, own_a, far_a, own_c, far_c, *refs):
        outs, both, weights, picked, sems = refs[:3], *refs[3:]
        core = core_ref[0]
        columns = pl.ds(pl.multiple_of(core * (modes // 2) + at, 128), width)
        copies = []
        for i, (a, c) in enumerate(((own_a, own_c), (far_a, far_c))):
            side = core if i == 0 else 1 - core
            nodes_here = pl.ds(pl.multiple_of(side * nodes, nodes), nodes)
            copies.append(pltpu.make_async_copy(a.at[:, columns], both.at[nodes_here, :], sems.at[2 * i]))
            copies.append(pltpu.make_async_copy(c, weights.at[side], sems.at[2 * i + 1]))
        for copy in copies:
            copy.start()
        for copy in copies:
            copy.wait()
        for out, pairs in zip(outs, lists):
            for place, (face, k) in enumerate(pairs):
                own = core == face
                for s in range(per):
                    slot = k * per + s
                    for n in range(depth // rows):
                        block = jnp.where(own, own_blocks[slot, n], far_blocks[slot, n])
                        first = pl.multiple_of(face * nodes + block * rows, rows)
                        picked[n * rows : (n + 1) * rows, :] = both[pl.ds(first, rows), :]
                    row = (place * per + s) * rows
                    out[row : row + rows, :] = jnp.dot(
                        weights[face, slot], picked[...], preferred_element_type=F32
                    ).astype(BF16)

    shapes = [(len(pairs) * per * rows, width) for pairs in lists]
    return call(
        coupled_rows,
        [core, *blocks],
        [in_hbm(acoustic[0]), acoustic[1], in_hbm(coupling[0]), coupling[1]],
        after,
        [jax.ShapeDtypeStruct(shape, BF16) for shape in shapes],
        [
            pltpu.VMEM((2 * nodes, width), BF16),
            pltpu.VMEM((2, *coupling[0].shape), BF16),
            pltpu.VMEM((depth, width), BF16),
            pltpu.SemaphoreType.DMA((4,)),
        ],
        fetched=4,
        time=2.5,
    )


def turned(struct_modes, after):
    depth, modes = struct_modes.shape
    step = 128 if modes % 128 == 0 else modes

    def turn(in_ref, out_ref):
        for i in range(0, modes, step):
            out_ref[i : i + step, :] = in_ref[:, i : i + step].T

    return call(
        turn, [], [struct_modes], after, [jax.ShapeDtypeStruct((modes, depth), BF16)], time=2.5
    )


def slots_of(core, shifts, per, after):
    count = shifts[0].shape[0]

    def slots(core_ref, own_shift, far_shift, out):
        for half, shift in enumerate((own_shift, far_shift)):
            first_core = core_ref[0] == half
            bases = [jnp.where(first_core, FOUND[0][k], FOUND[1][k]) * per for k in range(CLASSES)]
            for b in range(count):
                kind = shift[b]
                slot = jnp.int32(0)
                for k in range(CLASSES):
                    slot = jnp.where(kind == k, bases[k], slot)
                    bases[k] = bases[k] + (kind == k).astype(jnp.int32)
                out[half * count + b] = slot

    shape = jax.ShapeDtypeStruct((2 * count,), jnp.int32)
    return call(slots, [core, *shifts], [], after, [shape], scalar_out=True)


def panel(slots, here, bit, lefts, pieces, share, after):
    modes, depth = lefts[0].shape
    width = pieces[0].shape[1]
    count = slots.shape[0]
    rows = 2 * depth // count
    run = 2**bit * share
    tile = min(run, 256)

    def panel_part(slot_ref, here_ref, own, far, *refs):
        parts, away, kept, picked = refs[:3], refs[3], refs[4], refs[5]
        for b in range(count):
            slot = slot_ref[b]
            base = 0
            for part in parts:
                many = part.shape[0] // rows

                @pl.when((slot >= base) & (slot < base + many))
                def _(part=part, b=b, slot=slot, base=base):
                    first = pl.multiple_of((slot - base) * rows, rows)
                    picked[b * rows : (b + 1) * rows, :] = part[pl.ds(first, rows), :]

                base += many
        for out, side in ((away, 1 - here_ref[0]), (kept, here_ref[0])):

            @pl.loop(0, modes // 2 // tile)
            def _(i, out=out, side=side):
                at = i * tile
                first = (at // run * 2 + side) * run + at % run
                taken = pl.ds(pl.multiple_of(first, tile), tile)
                product = jnp.dot(own[taken, :], picked[:depth, :], preferred_element_type=F32)
                product += jnp.dot(far[taken, :], picked[depth:, :], preferred_element_type=F32)
                out[pl.ds(pl.multiple_of(at, tile), tile), :] = product.astype(out.dtype)

    return call(
        panel_part,
        [slots, here],
        [*lefts, *pieces],
        after,
        [
            jax.ShapeDtypeStruct((modes // 2, width), BF16),
            jax.ShapeDtypeStruct((modes // 2, width), F32),
        ],
        [pltpu.VMEM((2 * depth, width), BF16)],
        time=4.0,
    )


def added(held, got, here, before, wire, after):
    width = held.shape[1]
    shape = (before, 2, held.shape[0] // before // 2, width)
    tall = shape[2]
    each = before // len(got)

    def added_split(here_ref, held_ref, *refs):
        kept_ref, away_ref = refs[-2:]
        side = here_ref[0]
        for i in range(before):
            at = slice(i * tall, (i + 1) * tall)
            arrived = refs[i // each]
            kept_ref[at, :] = held_ref[i, side] + arrived[i % each, side].astype(F32)
            away = held_ref[i, 1 - side] + arrived[i % each, 1 - side].astype(F32)
            away_ref[at, :] = away.astype(wire)

    out = (before * tall, width)
    return call(
        added_split,
        [here],
        [held.reshape(shape), *[block.reshape(each, *shape[1:]) for block in got]],
        after,
        [jax.ShapeDtypeStruct(out, F32), jax.ShapeDtypeStruct(out, wire)],
    )


def together(core, own, far, starts, modes):
    rows = own[0].shape[0]

    def put_together(core_ref, *refs):
        out = refs[-1]
        for half, blocks in enumerate((refs[: len(own)], refs[len(own) : -1])):
            side = core_ref[0] if half == 0 else 1 - core_ref[0]
            for at, block in zip(starts, blocks):
                first = pl.multiple_of(side * (modes // 2) + at, 128)
                out[:, pl.ds(first, block.shape[1])] = block[...]

    out, _ = call(put_together, [core], [*own, *far], [], [jax.ShapeDtypeStruct((rows, modes), F32)])
    return out


def passed_along(block, distance):
    size = lax.axis_size("mesh")
    return lax.ppermute(block, "mesh", [((i - distance) % size, i) for i in range(size)])


def swapped(block, bit):
    size = lax.axis_size("mesh")
    return lax.ppermute(block, "mesh", [(i, i ^ (1 << bit)) for i in range(size)])


def planned(levels):
    chunks = len(UNITS)
    steps = [("coupled", 0), ("turned", 0), *(("coupled", j) for j in range(1, EARLY))]
    for now in range(chunks + levels):
        steps.append(("panel", now))
        steps.extend((level, now - level) for level in range(1, levels + 1))
        steps.append(("coupled", now + EARLY))
    return [step for step in steps if 0 <= step[1] < chunks]


def per_device(struct_modes, acoustic_modes, coupling, face_shift, face_blocks):
    size = lax.axis_size("mesh")
    me = lax.axis_index("mesh")
    modes = acoustic_modes.shape[1]
    share = struct_modes.shape[1] // size
    bits = list(range(1, size.bit_length() - 1))
    first = ORDERS
    levels = len(bits)
    orders = [[*(first[j] if j in first else [2, 1, 3]), *bits[3:]] for j in range(len(UNITS))]
    widths = [units * (modes // 2 // sum(UNITS)) for units in UNITS]
    starts = [sum(widths[:j]) for j in range(len(widths))]

    def bit_of(bit):
        return ((me >> bit) & 1).reshape(1)

    core = bit_of(0)
    token = []
    blocks = (face_blocks, swapped(face_blocks, 0))
    couplings = (coupling, swapped(coupling, 0))
    acoustics = (acoustic_modes, swapped(acoustic_modes, 0))
    shifts = (face_shift, swapped(face_shift, 0))
    per = coupling.shape[0] // CLASSES
    state = [dict(bits=sorted([0, *order[1:]], reverse=True)) for order in orders]
    finished = []
    for stage, j in planned(levels):
        now, order = state[j], orders[j]
        if stage == "coupled":
            ahead, behind, here, last = coupled(
                core, blocks, acoustics, couplings, starts[j], widths[j], token
            )
            now["pieces"] = [passed_along(ahead, 2), passed_along(behind, -2), here]
            if j == 0:
                later, _ = lax.optimization_barrier((struct_modes, last))
                now["far"] = swapped(later, 0)
        elif stage == "turned":
            own, last = turned(struct_modes, token)
            slots, last = slots_of(core, shifts, per, [last])
            far, last = turned(now["far"], [last])
        elif stage == "panel":
            bit = order[0]
            away, now["held"], last = panel(
                slots, bit_of(bit), bit, (own, far), now["pieces"], share, token
            )
            now["got"] = [swapped(away, bit)]
        else:
            bit = order[stage] if stage < levels else 0
            place = now["bits"].index(bit)
            now["bits"].remove(bit)
            wire = BF16 if stage < min(levels, 3) else F32
            now["held"], away, last = added(
                now["held"], now["got"], bit_of(bit), 2**place, wire, token
            )
            now["got"] = [swapped(away, bit)]
        token = [last]
    return together(
        core, [now["held"] for now in state], [now["got"][0] for now in state], starts, modes
    )


def solution(mesh):
    placed = (
        P(("member", "mesh"), None),
        P(("member", "mesh"), None),
        P("mesh", None, None),
        P("mesh"),
        P("mesh", None),
    )
    return jax.shard_map(
        per_device,
        mesh=mesh,
        in_specs=placed,
        out_specs=P(("member", "mesh"), None),
        check_vma=False,
    )
```

```python
import jax
import jax.numpy as jnp
from jax import lax
from jax.experimental import pallas as pl
from jax.experimental.pallas import tpu as pltpu
from jax.sharding import PartitionSpec as P

CLASSES = 5
UNITS = (2, 2, 3, 1)
EARLY = 4
ORDERS = {3: [1, 2, 3]}
PACE = 10**10
LIMIT = 8 * 2**20
ANY = pl.BlockSpec(memory_space=pl.ANY)
BF16, F32 = jnp.bfloat16, jnp.float32
NEXT = ((0, 0), (1, 0), (1, 1))
BEFORE = ((0, 3), (0, 4), (1, 4))
HERE = ((0, 1), (0, 2), (1, 2), (1, 3))
FOUND = ((0, 2, 7, 9, 4), (1, 6, 8, 3, 5))


def call(body, scalars, arrays, after, out_shape, scratch=(), fetched=0, scalar_out=False, time=1.0):
    lead = len(scalars) + len(arrays)
    extra = len(after)
    outs = len(out_shape)

    def kernel(*refs):
        rest = refs[lead + extra :]
        body(*refs[:lead], *rest[:outs], *rest[outs + 1 :])

    kernel.__name__ = body.__name__
    vmem, smem = (pl.BlockSpec(memory_space=space) for space in (pltpu.VMEM, pltpu.SMEM))
    return pl.pallas_call(
        kernel,
        out_shape=[*out_shape, jax.ShapeDtypeStruct((8, 128), F32)],
        in_specs=[smem] * len(scalars)
        + ([ANY] * fetched or [vmem] * len(arrays))
        + [ANY] * extra,
        out_specs=[smem if scalar_out else vmem] * outs + [ANY],
        scratch_shapes=scratch,
        compiler_params=pltpu.CompilerParams(vmem_limit_bytes=LIMIT),
        cost_estimate=pl.CostEstimate(flops=int(time * PACE), bytes_accessed=1, transcendentals=0),
        name=body.__name__,
    )(*scalars, *arrays, *after)


def in_hbm(array):
    return pltpu.with_memory_space_constraint(array, pltpu.HBM)


def coupled(core, blocks, acoustic, coupling, at, width, after):
    slots, rows, depth = coupling[0].shape
    per = slots // CLASSES
    nodes, modes = acoustic[0].shape
    lists = (NEXT, BEFORE, HERE)

    def coupled_rows(core_ref, own_blocks, far_blocks, own_a, far_a, own_c, far_c, *refs):
        outs, both, weights, picked, sems = refs[:3], *refs[3:]
        core = core_ref[0]
        columns = pl.ds(pl.multiple_of(core * (modes // 2) + at, 128), width)
        copies = []
        for i, (a, c) in enumerate(((own_a, own_c), (far_a, far_c))):
            side = core if i == 0 else 1 - core
            nodes_here = pl.ds(pl.multiple_of(side * nodes, nodes), nodes)
            copies.append(pltpu.make_async_copy(a.at[:, columns], both.at[nodes_here, :], sems.at[2 * i]))
            copies.append(pltpu.make_async_copy(c, weights.at[side], sems.at[2 * i + 1]))
        for copy in copies:
            copy.start()
        for copy in copies:
            copy.wait()
        for out, pairs in zip(outs, lists):
            for place, (face, k) in enumerate(pairs):
                own = core == face
                for s in range(per):
                    slot = k * per + s
                    for n in range(depth // rows):
                        block = jnp.where(own, own_blocks[slot, n], far_blocks[slot, n])
                        first = pl.multiple_of(face * nodes + block * rows, rows)
                        picked[n * rows : (n + 1) * rows, :] = both[pl.ds(first, rows), :]
                    row = (place * per + s) * rows
                    out[row : row + rows, :] = jnp.dot(
                        weights[face, slot], picked[...], preferred_element_type=F32
                    ).astype(BF16)

    shapes = [(len(pairs) * per * rows, width) for pairs in lists]
    return call(
        coupled_rows,
        [core, *blocks],
        [in_hbm(acoustic[0]), acoustic[1], in_hbm(coupling[0]), coupling[1]],
        after,
        [jax.ShapeDtypeStruct(shape, BF16) for shape in shapes],
        [
            pltpu.VMEM((2 * nodes, width), BF16),
            pltpu.VMEM((2, *coupling[0].shape), BF16),
            pltpu.VMEM((depth, width), BF16),
            pltpu.SemaphoreType.DMA((4,)),
        ],
        fetched=4,
        time=2.5,
    )


def turned(struct_modes, after):
    depth, modes = struct_modes.shape
    step = 128 if modes % 128 == 0 else modes

    def turn(in_ref, out_ref):
        for i in range(0, modes, step):
            out_ref[i : i + step, :] = in_ref[:, i : i + step].T

    return call(
        turn, [], [struct_modes], after, [jax.ShapeDtypeStruct((modes, depth), BF16)], time=2.5
    )


def slots_of(core, shifts, per, after):
    count = shifts[0].shape[0]

    def slots(core_ref, own_shift, far_shift, out):
        for half, shift in enumerate((own_shift, far_shift)):
            first_core = core_ref[0] == half
            bases = [jnp.where(first_core, FOUND[0][k], FOUND[1][k]) * per for k in range(CLASSES)]
            for b in range(count):
                kind = shift[b]
                slot = jnp.int32(0)
                for k in range(CLASSES):
                    slot = jnp.where(kind == k, bases[k], slot)
                    bases[k] = bases[k] + (kind == k).astype(jnp.int32)
                out[half * count + b] = slot

    shape = jax.ShapeDtypeStruct((2 * count,), jnp.int32)
    return call(slots, [core, *shifts], [], after, [shape], scalar_out=True)


def panel(slots, here, bit, lefts, pieces, share, after):
    modes, depth = lefts[0].shape
    width = pieces[0].shape[1]
    count = slots.shape[0]
    rows = 2 * depth // count
    run = 2**bit * share
    tile = min(run, 256)

    def multiply(out, side, own, far, picked):
        @pl.loop(0, modes // 2 // tile)
        def _(i):
            at = i * tile
            first = (at // run * 2 + side) * run + at % run
            taken = pl.ds(pl.multiple_of(first, tile), tile)
            product = jnp.dot(own[taken, :], picked[:depth, :], preferred_element_type=F32)
            product += jnp.dot(far[taken, :], picked[depth:, :], preferred_element_type=F32)
            out[pl.ds(pl.multiple_of(at, tile), tile), :] = product.astype(out.dtype)

    def panel_away(slot_ref, here_ref, own, far, *refs):
        parts, away, picked = refs[:3], refs[3], refs[4]
        for b in range(count):
            slot = slot_ref[b]
            base = 0
            for part in parts:
                many = part.shape[0] // rows

                @pl.when((slot >= base) & (slot < base + many))
                def _(part=part, b=b, slot=slot, base=base):
                    first = pl.multiple_of((slot - base) * rows, rows)
                    picked[b * rows : (b + 1) * rows, :] = part[pl.ds(first, rows), :]

                base += many
        multiply(away, 1 - here_ref[0], own, far, picked)

    def panel_own(here_ref, own, far, picked, kept):
        multiply(kept, here_ref[0], own, far, picked)

    half = (modes // 2, width)
    away, picked, last = call(
        panel_away,
        [slots, here],
        [*lefts, *pieces],
        after,
        [jax.ShapeDtypeStruct(half, BF16), jax.ShapeDtypeStruct((2 * depth, width), BF16)],
        time=5.0,
    )
    kept, last = call(
        panel_own, [here], [*lefts, picked], [last], [jax.ShapeDtypeStruct(half, F32)], time=1.5
    )
    return away, kept, last


def added(held, got, here, before, wire, after):
    width = held.shape[1]
    shape = (before, 2, held.shape[0] // before // 2, width)
    tall = shape[2]
    each = before // len(got)

    def added_split(here_ref, held_ref, *refs):
        kept_ref, away_ref = refs[-2:]
        side = here_ref[0]
        for i in range(before):
            at = slice(i * tall, (i + 1) * tall)
            arrived = refs[i // each]
            kept_ref[at, :] = held_ref[i, side] + arrived[i % each, side].astype(F32)
            away = held_ref[i, 1 - side] + arrived[i % each, 1 - side].astype(F32)
            away_ref[at, :] = away.astype(wire)

    out = (before * tall, width)
    return call(
        added_split,
        [here],
        [held.reshape(shape), *[block.reshape(each, *shape[1:]) for block in got]],
        after,
        [jax.ShapeDtypeStruct(out, F32), jax.ShapeDtypeStruct(out, wire)],
    )


def together(core, own, far, starts, modes):
    rows = own[0].shape[0]

    def put_together(core_ref, *refs):
        out = refs[-1]
        for half, blocks in enumerate((refs[: len(own)], refs[len(own) : -1])):
            side = core_ref[0] if half == 0 else 1 - core_ref[0]
            for at, block in zip(starts, blocks):
                first = pl.multiple_of(side * (modes // 2) + at, 128)
                out[:, pl.ds(first, block.shape[1])] = block[...]

    out, _ = call(put_together, [core], [*own, *far], [], [jax.ShapeDtypeStruct((rows, modes), F32)])
    return out


def passed_along(block, distance):
    size = lax.axis_size("mesh")
    return lax.ppermute(block, "mesh", [((i - distance) % size, i) for i in range(size)])


def swapped(block, bit):
    size = lax.axis_size("mesh")
    return lax.ppermute(block, "mesh", [(i, i ^ (1 << bit)) for i in range(size)])


def planned(levels):
    chunks = len(UNITS)
    steps = [("coupled", 0), ("turned", 0), *(("coupled", j) for j in range(1, EARLY))]
    for now in range(chunks + levels):
        steps.append(("panel", now))
        steps.extend((level, now - level) for level in range(1, levels + 1))
        steps.append(("coupled", now + EARLY))
    return [step for step in steps if 0 <= step[1] < chunks]


def per_device(struct_modes, acoustic_modes, coupling, face_shift, face_blocks):
    size = lax.axis_size("mesh")
    me = lax.axis_index("mesh")
    modes = acoustic_modes.shape[1]
    share = struct_modes.shape[1] // size
    bits = list(range(1, size.bit_length() - 1))
    first = ORDERS
    levels = len(bits)
    orders = [[*(first[j] if j in first else [2, 1, 3]), *bits[3:]] for j in range(len(UNITS))]
    widths = [units * (modes // 2 // sum(UNITS)) for units in UNITS]
    starts = [sum(widths[:j]) for j in range(len(widths))]

    def bit_of(bit):
        return ((me >> bit) & 1).reshape(1)

    core = bit_of(0)
    token = []
    blocks = (face_blocks, swapped(face_blocks, 0))
    couplings = (coupling, swapped(coupling, 0))
    acoustics = (acoustic_modes, swapped(acoustic_modes, 0))
    shifts = (face_shift, swapped(face_shift, 0))
    per = coupling.shape[0] // CLASSES
    state = [dict(bits=sorted([0, *order[1:]], reverse=True)) for order in orders]
    finished = []
    for stage, j in planned(levels):
        now, order = state[j], orders[j]
        if stage == "coupled":
            ahead, behind, here, last = coupled(
                core, blocks, acoustics, couplings, starts[j], widths[j], token
            )
            now["pieces"] = [passed_along(ahead, 2), passed_along(behind, -2), here]
            if j == 0:
                later, _ = lax.optimization_barrier((struct_modes, last))
                now["far"] = swapped(later, 0)
        elif stage == "turned":
            own, last = turned(struct_modes, token)
            slots, last = slots_of(core, shifts, per, [last])
            far, last = turned(now["far"], [last])
        elif stage == "panel":
            bit = order[0]
            away, now["held"], last = panel(
                slots, bit_of(bit), bit, (own, far), now["pieces"], share, token
            )
            now["got"] = [swapped(away, bit)]
        else:
            bit = order[stage] if stage < levels else 0
            place = now["bits"].index(bit)
            now["bits"].remove(bit)
            wire = BF16 if stage < min(levels, 3) else F32
            now["held"], away, last = added(
                now["held"], now["got"], bit_of(bit), 2**place, wire, token
            )
            now["got"] = [swapped(away, bit)]
        token = [last]
    return together(
        core, [now["held"] for now in state], [now["got"][0] for now in state], starts, modes
    )


def solution(mesh):
    placed = (
        P(("member", "mesh"), None),
        P(("member", "mesh"), None),
        P("mesh", None, None),
        P("mesh"),
        P("mesh", None),
    )
    return jax.shard_map(
        per_device,
        mesh=mesh,
        in_specs=placed,
        out_specs=P(("member", "mesh"), None),
        check_vma=False,
    )
```

```python
import jax
import jax.numpy as jnp
from jax import lax
from jax.experimental import pallas as pl
from jax.experimental.pallas import tpu as pltpu
from jax.sharding import PartitionSpec as P

CLASSES = 5
UNITS = (2, 2, 2, 2)
EARLY = 4
ORDERS = {3: [1, 2, 3]}
PACE = 10**10
LIMIT = 8 * 2**20
ANY = pl.BlockSpec(memory_space=pl.ANY)
BF16, F32 = jnp.bfloat16, jnp.float32
NEXT = ((0, 0), (1, 0), (1, 1))
BEFORE = ((0, 3), (0, 4), (1, 4))
HERE = ((0, 1), (0, 2), (1, 2), (1, 3))
FOUND = ((0, 2, 7, 9, 4), (1, 6, 8, 3, 5))


def call(body, scalars, arrays, after, out_shape, scratch=(), fetched=0, scalar_out=False, time=1.0):
    lead = len(scalars) + len(arrays)
    extra = len(after)
    outs = len(out_shape)

    def kernel(*refs):
        rest = refs[lead + extra :]
        body(*refs[:lead], *rest[:outs], *rest[outs + 1 :])

    kernel.__name__ = body.__name__
    vmem, smem = (pl.BlockSpec(memory_space=space) for space in (pltpu.VMEM, pltpu.SMEM))
    return pl.pallas_call(
        kernel,
        out_shape=[*out_shape, jax.ShapeDtypeStruct((8, 128), F32)],
        in_specs=[smem] * len(scalars)
        + ([ANY] * fetched or [vmem] * len(arrays))
        + [ANY] * extra,
        out_specs=[smem if scalar_out else vmem] * outs + [ANY],
        scratch_shapes=scratch,
        compiler_params=pltpu.CompilerParams(vmem_limit_bytes=LIMIT),
        cost_estimate=pl.CostEstimate(flops=int(time * PACE), bytes_accessed=1, transcendentals=0),
        name=body.__name__,
    )(*scalars, *arrays, *after)


def in_hbm(array):
    return pltpu.with_memory_space_constraint(array, pltpu.HBM)


def coupled(core, blocks, acoustic, coupling, at, width, after):
    slots, rows, depth = coupling[0].shape
    per = slots // CLASSES
    nodes, modes = acoustic[0].shape
    lists = (NEXT, BEFORE, HERE)

    def coupled_rows(core_ref, own_blocks, far_blocks, own_a, far_a, own_c, far_c, *refs):
        outs, both, weights, picked, sems = refs[:3], *refs[3:]
        core = core_ref[0]
        columns = pl.ds(pl.multiple_of(core * (modes // 2) + at, 128), width)
        copies = []
        for i, (a, c) in enumerate(((own_a, own_c), (far_a, far_c))):
            side = core if i == 0 else 1 - core
            nodes_here = pl.ds(pl.multiple_of(side * nodes, nodes), nodes)
            copies.append(pltpu.make_async_copy(a.at[:, columns], both.at[nodes_here, :], sems.at[2 * i]))
            copies.append(pltpu.make_async_copy(c, weights.at[side], sems.at[2 * i + 1]))
        for copy in copies:
            copy.start()
        for copy in copies:
            copy.wait()
        for out, pairs in zip(outs, lists):
            for place, (face, k) in enumerate(pairs):
                own = core == face
                for s in range(per):
                    slot = k * per + s
                    for n in range(depth // rows):
                        block = jnp.where(own, own_blocks[slot, n], far_blocks[slot, n])
                        first = pl.multiple_of(face * nodes + block * rows, rows)
                        picked[n * rows : (n + 1) * rows, :] = both[pl.ds(first, rows), :]
                    row = (place * per + s) * rows
                    out[row : row + rows, :] = jnp.dot(
                        weights[face, slot], picked[...], preferred_element_type=F32
                    ).astype(BF16)

    shapes = [(len(pairs) * per * rows, width) for pairs in lists]
    return call(
        coupled_rows,
        [core, *blocks],
        [in_hbm(acoustic[0]), acoustic[1], in_hbm(coupling[0]), coupling[1]],
        after,
        [jax.ShapeDtypeStruct(shape, BF16) for shape in shapes],
        [
            pltpu.VMEM((2 * nodes, width), BF16),
            pltpu.VMEM((2, *coupling[0].shape), BF16),
            pltpu.VMEM((depth, width), BF16),
            pltpu.SemaphoreType.DMA((4,)),
        ],
        fetched=4,
        time=2.5,
    )


def turned(struct_modes, after):
    depth, modes = struct_modes.shape
    step = 128 if modes % 128 == 0 else modes

    def turn(in_ref, out_ref):
        for i in range(0, modes, step):
            out_ref[i : i + step, :] = in_ref[:, i : i + step].T

    return call(
        turn, [], [struct_modes], after, [jax.ShapeDtypeStruct((modes, depth), BF16)], time=2.5
    )


def slots_of(core, shifts, per, after):
    count = shifts[0].shape[0]

    def slots(core_ref, own_shift, far_shift, out):
        for half, shift in enumerate((own_shift, far_shift)):
            first_core = core_ref[0] == half
            bases = [jnp.where(first_core, FOUND[0][k], FOUND[1][k]) * per for k in range(CLASSES)]
            for b in range(count):
                kind = shift[b]
                slot = jnp.int32(0)
                for k in range(CLASSES):
                    slot = jnp.where(kind == k, bases[k], slot)
                    bases[k] = bases[k] + (kind == k).astype(jnp.int32)
                out[half * count + b] = slot

    shape = jax.ShapeDtypeStruct((2 * count,), jnp.int32)
    return call(slots, [core, *shifts], [], after, [shape], scalar_out=True)


def panel(slots, here, bit, lefts, pieces, share, after):
    modes, depth = lefts[0].shape
    width = pieces[0].shape[1]
    count = slots.shape[0]
    rows = 2 * depth // count
    run = 2**bit * share
    tile = min(run, 256)

    def multiply(out, side, own, far, picked):
        @pl.loop(0, modes // 2 // tile)
        def _(i):
            at = i * tile
            first = (at // run * 2 + side) * run + at % run
            taken = pl.ds(pl.multiple_of(first, tile), tile)
            product = jnp.dot(own[taken, :], picked[:depth, :], preferred_element_type=F32)
            product += jnp.dot(far[taken, :], picked[depth:, :], preferred_element_type=F32)
            out[pl.ds(pl.multiple_of(at, tile), tile), :] = product.astype(out.dtype)

    def panel_away(slot_ref, here_ref, own, far, *refs):
        parts, away, picked = refs[:3], refs[3], refs[4]
        for b in range(count):
            slot = slot_ref[b]
            base = 0
            for part in parts:
                many = part.shape[0] // rows

                @pl.when((slot >= base) & (slot < base + many))
                def _(part=part, b=b, slot=slot, base=base):
                    first = pl.multiple_of((slot - base) * rows, rows)
                    picked[b * rows : (b + 1) * rows, :] = part[pl.ds(first, rows), :]

                base += many
        multiply(away, 1 - here_ref[0], own, far, picked)

    def panel_own(here_ref, own, far, picked, kept):
        multiply(kept, here_ref[0], own, far, picked)

    half = (modes // 2, width)
    away, picked, last = call(
        panel_away,
        [slots, here],
        [*lefts, *pieces],
        after,
        [jax.ShapeDtypeStruct(half, BF16), jax.ShapeDtypeStruct((2 * depth, width), BF16)],
        time=5.0,
    )
    kept, last = call(
        panel_own, [here], [*lefts, picked], [last], [jax.ShapeDtypeStruct(half, F32)], time=1.5
    )
    return away, kept, last


def added(held, got, here, before, wire, after):
    width = held.shape[1]
    shape = (before, 2, held.shape[0] // before // 2, width)
    tall = shape[2]
    each = before // len(got)

    def added_split(here_ref, held_ref, *refs):
        kept_ref, away_ref = refs[-2:]
        side = here_ref[0]
        for i in range(before):
            at = slice(i * tall, (i + 1) * tall)
            arrived = refs[i // each]
            kept_ref[at, :] = held_ref[i, side] + arrived[i % each, side].astype(F32)
            away = held_ref[i, 1 - side] + arrived[i % each, 1 - side].astype(F32)
            away_ref[at, :] = away.astype(wire)

    out = (before * tall, width)
    return call(
        added_split,
        [here],
        [held.reshape(shape), *[block.reshape(each, *shape[1:]) for block in got]],
        after,
        [jax.ShapeDtypeStruct(out, F32), jax.ShapeDtypeStruct(out, wire)],
    )


def together(core, own, far, starts, modes):
    rows = own[0].shape[0]

    def put_together(core_ref, *refs):
        out = refs[-1]
        for half, blocks in enumerate((refs[: len(own)], refs[len(own) : -1])):
            side = core_ref[0] if half == 0 else 1 - core_ref[0]
            for at, block in zip(starts, blocks):
                first = pl.multiple_of(side * (modes // 2) + at, 128)
                out[:, pl.ds(first, block.shape[1])] = block[...]

    out, _ = call(put_together, [core], [*own, *far], [], [jax.ShapeDtypeStruct((rows, modes), F32)])
    return out


def passed_along(block, distance):
    size = lax.axis_size("mesh")
    return lax.ppermute(block, "mesh", [((i - distance) % size, i) for i in range(size)])


def swapped(block, bit):
    size = lax.axis_size("mesh")
    return lax.ppermute(block, "mesh", [(i, i ^ (1 << bit)) for i in range(size)])


def planned(levels):
    chunks = len(UNITS)
    steps = [("coupled", 0), ("turned", 0), *(("coupled", j) for j in range(1, EARLY))]
    for now in range(chunks + levels):
        steps.append(("panel", now))
        steps.extend((level, now - level) for level in range(1, levels + 1))
        steps.append(("coupled", now + EARLY))
    return [step for step in steps if 0 <= step[1] < chunks]


def per_device(struct_modes, acoustic_modes, coupling, face_shift, face_blocks):
    size = lax.axis_size("mesh")
    me = lax.axis_index("mesh")
    modes = acoustic_modes.shape[1]
    share = struct_modes.shape[1] // size
    bits = list(range(1, size.bit_length() - 1))
    first = ORDERS
    levels = len(bits)
    orders = [[*(first[j] if j in first else [2, 1, 3]), *bits[3:]] for j in range(len(UNITS))]
    widths = [units * (modes // 2 // sum(UNITS)) for units in UNITS]
    starts = [sum(widths[:j]) for j in range(len(widths))]

    def bit_of(bit):
        return ((me >> bit) & 1).reshape(1)

    core = bit_of(0)
    token = []
    blocks = (face_blocks, swapped(face_blocks, 0))
    couplings = (coupling, swapped(coupling, 0))
    acoustics = (acoustic_modes, swapped(acoustic_modes, 0))
    shifts = (face_shift, swapped(face_shift, 0))
    per = coupling.shape[0] // CLASSES
    state = [dict(bits=sorted([0, *order[1:]], reverse=True)) for order in orders]
    finished = []
    for stage, j in planned(levels):
        now, order = state[j], orders[j]
        if stage == "coupled":
            ahead, behind, here, last = coupled(
                core, blocks, acoustics, couplings, starts[j], widths[j], token
            )
            now["pieces"] = [passed_along(ahead, 2), passed_along(behind, -2), here]
            if j == 0:
                later, _ = lax.optimization_barrier((struct_modes, last))
                now["far"] = swapped(later, 0)
        elif stage == "turned":
            own, last = turned(struct_modes, token)
            slots, last = slots_of(core, shifts, per, [last])
            far, last = turned(now["far"], [last])
        elif stage == "panel":
            bit = order[0]
            away, now["held"], last = panel(
                slots, bit_of(bit), bit, (own, far), now["pieces"], share, token
            )
            now["got"] = [swapped(away, bit)]
        else:
            bit = order[stage] if stage < levels else 0
            place = now["bits"].index(bit)
            now["bits"].remove(bit)
            wire = BF16 if stage < min(levels, 3) else F32
            now["held"], away, last = added(
                now["held"], now["got"], bit_of(bit), 2**place, wire, token
            )
            now["got"] = [swapped(away, bit)]
        token = [last]
    return together(
        core, [now["held"] for now in state], [now["got"][0] for now in state], starts, modes
    )


def solution(mesh):
    placed = (
        P(("member", "mesh"), None),
        P(("member", "mesh"), None),
        P("mesh", None, None),
        P("mesh"),
        P("mesh", None),
    )
    return jax.shard_map(
        per_device,
        mesh=mesh,
        in_specs=placed,
        out_specs=P(("member", "mesh"), None),
        check_vma=False,
    )
```
